256 devices in a mesh: dom: 32 (over y, x, z_lo), cls: 8 (over z_hi, core).
Axes of the slice: x: 4, y: 4, z: 8 (z_hi: 4, z_lo: 2; z = z_hi * 2 + z_lo), core: 2. Of those that a mesh axis runs over, the one named last changes fastest.
Arguments:
- particles: bfloat16 [8192, 2, 4096], P(('dom', 'cls')), may hold values from -1200 to 1200
- defocus: bfloat16 [8192], P(('dom', 'cls')), may hold values from 1.2 to 3
- orient: int32 [8192, 16], P(('dom', 'cls')), may hold values from 0 to 47, as said below
- center: int32 [8192], P(('dom', 'cls')), may hold values from 0 to 48
- live: int32 [256], P(('dom', 'cls')), may hold values from 1 to 32, 4096 in all
- sigma2: float32 [4096], replicated, may hold values from 400 to 3000
- projections: bfloat16 [8, 48, 2, 4096], P('cls', None, None, 'dom'), may hold values from -5 to 5
Outputs:
- estimate: float32 [8, 48, 2, 4096], P('cls', None, None, 'dom')
- log_evidence: float32 [8192], P(('dom', 'cls'))
The draws below stay inside these ranges and needn't reach their ends.
Inputs may be any that keep to these rules, and one draw needn't show every extreme that they name: `orient`: each row holds 16 different orientation indices. live particles fill the first slots of a device; some device is full.
All inputs are finite; a program needn't handle non-finite values.
Results may differ from the reference program's by a relative error of at most 0.003.
Values may be sent and summed in bfloat16 or wider, within the bound.
A program may use at most 256 MiB of HBM per device.

```python
import math
import jax
import jax.numpy as jnp
import numpy as np
from jax import lax

FSIDE = 64
FREQ = 4096
BOX = 128
GRID = 9
SHIFTS = 9
ORIENTS = 48
CANDS = 16
SLAB = 32
CLASSES = 8
PARTICLES = 8192
N_DOM = 32
N_CLS = 8


def common(key):
    class_key = jax.random.fold_in(key, 101)
    orient_key = jax.random.fold_in(key, 102)
    center_key = jax.random.fold_in(key, 103)
    defocus_key = jax.random.fold_in(key, 104)
    volume_key = jax.random.fold_in(key, 105)
    classes = jax.random.randint(class_key, (PARTICLES,), 0, CLASSES)
    ranking = jax.random.randint(orient_key, (PARTICLES, ORIENTS), 0, 1 << 20) * ORIENTS + jnp.arange(ORIENTS, dtype=jnp.int32)[None, :]
    orient = lax.top_k(ranking, CANDS)[1].astype(jnp.int32)
    center = jax.random.randint(center_key, (PARTICLES,), 0, (GRID - 2) * (GRID - 2)).astype(jnp.int32)
    defocus = jnp.exp(math.log(1.2) + jax.random.uniform(defocus_key, (PARTICLES,), jnp.float32) * math.log(2.5))
    volumes = jnp.clip(jax.random.normal(volume_key, (CLASSES, ORIENTS, 2, FREQ), jnp.float32), -5.0, 5.0)
    return (classes, orient, center, defocus, volumes)


def draw_orient(key, part):
    return common(key)[1]


def draw_center(key, part):
    return common(key)[2]


def draw_defocus(key, part):
    return common(key)[3].astype(jnp.bfloat16)


def draw_projections(key, part):
    return common(key)[4].astype(jnp.bfloat16)


def draw_particles(key, part):
    classes, orient, center, defocus, volumes = common(key)
    key = jax.random.fold_in(key, 7)
    noise_key, amp_key = jax.random.split(key, 2)
    position = jnp.arange(FREQ, dtype=jnp.int32)
    freq_x = (position % FSIDE).astype(jnp.float32)
    freq_y = (position // FSIDE - FSIDE // 2).astype(jnp.float32)
    radius_sq = (freq_x * freq_x + freq_y * freq_y) / (BOX * BOX)
    contrast = -jnp.sin(400.0 * defocus[:, None] * radius_sq[None, :] + 0.07)
    inner_side = GRID - 2
    shift_x = (center % inner_side + 1 - GRID // 2).astype(jnp.float32)
    shift_y = (center // inner_side + 1 - GRID // 2).astype(jnp.float32)
    phase_angle = 2.0 * math.pi / BOX * (shift_x[:, None] * freq_x[None, :] + shift_y[:, None] * freq_y[None, :])
    cosine = jnp.cos(phase_angle)
    sine_part = jnp.sin(phase_angle)
    first_view = volumes[classes, orient[:, 0]]
    low_amplitude = 0.7 + 1.3 * jax.random.uniform(amp_key, (PARTICLES,), jnp.float32)
    amplitude = low_amplitude
    noise_field = 35.0 * jnp.clip(jax.random.normal(noise_key, (PARTICLES, 2, FREQ), jnp.float32), -6.0, 6.0)
    signal = amplitude[:, None, None] * first_view
    signal_real = contrast * signal[:, 0, :]
    signal_imag = contrast * signal[:, 1, :]
    real_part = signal_real * cosine + signal_imag * sine_part
    imag_part = signal_imag * cosine - signal_real * sine_part
    return (jnp.stack([real_part, imag_part], axis=1) + noise_field).astype(jnp.bfloat16)


def length_profile(number_of, total, most, skew):
    weights = [(1 << 20) // math.isqrt(standing ** skew) + 1 for standing in range(2, number_of + 1)]
    rest, holding = total - most - (number_of - 1), [1] * (number_of - 1)
    while rest > 0:
        candidates = [i for i in range(number_of - 1) if holding[i] < most]
        pool, left = sum([weights[i] for i in candidates]), rest
        for i in candidates:
            extra = min(most - holding[i], max(1, left * weights[i] // pool), rest)
            holding[i] = holding[i] + extra
            rest = rest - extra
    return np.array([most] + holding)


def uneven(own_key, number_of, total, reach, slope):
    if number_of == 2:
        one = jax.random.randint(own_key, (), max(1, total - reach), min(reach, total - 1) + 1)
        return jnp.stack([one, total - one])
    sizes = jnp.asarray(length_profile(number_of, total, reach, slope), jnp.int32)
    couples = (number_of - 1) // 2
    source_of, receiver = sizes[1:1 + 2 * couples:2], sizes[2:2 + 2 * couples:2]
    room = jnp.minimum(source_of - 1, reach - receiver)
    moved = jax.random.randint(jax.random.fold_in(own_key, 1), (couples,), 0, 1 << 20) % (room + 1)
    sizes = sizes.at[1:1 + 2 * couples:2].set(source_of - moved).at[2:2 + 2 * couples:2].set(receiver + moved)
    return sizes[jax.random.permutation(jax.random.fold_in(own_key, 2), number_of)]


def setup_inputs(seed: int = 0) -> dict:
    seeds = jax.random.split(jax.random.key(seed), 8)
    particles = draw_particles(jax.random.fold_in(seeds[7], 71), 0)
    defocus = draw_defocus(jax.random.fold_in(seeds[7], 71), 0)
    orient = draw_orient(jax.random.fold_in(seeds[7], 71), 0)
    center = draw_center(jax.random.fold_in(seeds[7], 71), 0)
    live = uneven(seeds[4], N_DOM * N_CLS, PARTICLES // 2, SLAB, 2).astype(jnp.int32)
    sigma2 = jnp.clip(jnp.exp(jax.random.uniform(seeds[5], (FREQ,), jnp.float32, math.log(400.0), math.log(3000.0))), 400.0, 3000.0)
    projections = draw_projections(jax.random.fold_in(seeds[7], 71), 0)
    return {"particles": particles, "defocus": defocus, "orient": orient, "center": center, "live": live, "sigma2": sigma2, "projections": projections}


CTF_GAIN = 400.0
CTF_PHASE = 0.07
WIENER_TERM = 0.002


def frequency_axes():
    position = jnp.arange(FSIDE * FSIDE, dtype=jnp.int32)
    freq_x = (position % FSIDE).astype(jnp.float32)
    freq_y = (position // FSIDE - FSIDE // 2).astype(jnp.float32)
    return freq_x, freq_y


def shift_images(images, defocus, center, sigma2):
    freq_x, freq_y = frequency_axes()
    radius_sq = (freq_x * freq_x + freq_y * freq_y) / (BOX * BOX)
    contrast = -jnp.sin(CTF_GAIN * defocus.astype(jnp.float32)[:, None] * radius_sq[None, :] + CTF_PHASE)
    weighting = contrast / sigma2[None, :]
    ctf_weight = (contrast * contrast / sigma2[None, :]).astype(jnp.bfloat16)
    inner_side = GRID - 2
    base_x = center % inner_side + 1 - GRID // 2
    base_y = center // inner_side + 1 - GRID // 2
    offsets = jnp.arange(SHIFTS, dtype=jnp.int32)
    shift_x = (base_x[:, None] + offsets[None, :] % 3 - 1).astype(jnp.float32)
    shift_y = (base_y[:, None] + offsets[None, :] // 3 - 1).astype(jnp.float32)
    phase_angle = (2.0 * math.pi / BOX) * (shift_x[:, :, None] * freq_x[None, None, :] + shift_y[:, :, None] * freq_y[None, None, :])
    cosine = jnp.cos(phase_angle)
    sine_part = jnp.sin(phase_angle)
    real_part = images[:, 0, :].astype(jnp.float32)[:, None, :]
    imag_part = images[:, 1, :].astype(jnp.float32)[:, None, :]
    shifted_real = weighting[:, None, :] * (real_part * cosine - imag_part * sine_part)
    shifted_imag = weighting[:, None, :] * (real_part * sine_part + imag_part * cosine)
    shifted = jnp.stack([shifted_real, shifted_imag], axis=2).astype(jnp.bfloat16)
    return shifted, ctf_weight


def block_terms(volume_rows, power_rows, sigma2, images, defocus, center, orient, live_mask):
    shifted, ctf_weight = shift_images(images, defocus, center, sigma2)
    particles_here = images.shape[0]
    columns = volume_rows.shape[0]
    flat_rows = shifted.reshape(particles_here * SHIFTS, volume_rows.shape[1])
    correlation = jnp.dot(flat_rows, volume_rows.T, preferred_element_type=jnp.float32).reshape(particles_here, SHIFTS, columns)
    power_term = jnp.dot(ctf_weight, power_rows.T, preferred_element_type=jnp.float32)
    scores = correlation - 0.5 * power_term[:, None, :]
    orient_of = jnp.arange(columns, dtype=jnp.int32) % ORIENTS
    allowed = jnp.any(orient[:, :, None] == orient_of[None, None, :], axis=1)
    masked = jnp.where(allowed[:, None, :], scores, -jnp.inf)
    maximum = jnp.max(masked, axis=(1, 2))
    exponent = jnp.exp(masked - maximum[:, None, None])
    partition = jnp.sum(exponent, axis=(1, 2))
    evidence = jnp.where(live_mask, maximum + jnp.log(partition), 0.0)
    posterior = jnp.where(live_mask[:, None, None], exponent / partition[:, None, None], 0.0).astype(jnp.bfloat16)
    data_sum = jnp.dot(posterior.reshape(particles_here * SHIFTS, columns).T, flat_rows, preferred_element_type=jnp.float32)
    posterior_mass = jnp.sum(posterior.astype(jnp.float32), axis=1).astype(jnp.bfloat16)
    weight_sum = jnp.dot(posterior_mass.T, ctf_weight, preferred_element_type=jnp.float32)
    return data_sum, weight_sum, evidence


def reference(particles, defocus, orient, center, live, sigma2, projections):
    columns = CLASSES * ORIENTS
    volume_rows = projections.reshape(columns, 2 * FREQ)
    wide_volumes = projections.astype(jnp.float32)
    real_vol = wide_volumes[:, :, 0, :]
    imag_vol = wide_volumes[:, :, 1, :]
    power_rows = (real_vol * real_vol + imag_vol * imag_vol).astype(jnp.bfloat16).reshape(columns, FREQ)
    position = jnp.arange(PARTICLES, dtype=jnp.int32)
    live_slots = (position % SLAB) < live[position // SLAB]
    block_rows = math.gcd(SLAB, 64)
    blocks = PARTICLES // block_rows

    def scan_step(running, inputs):
        data_sum, weight_sum, evidence = block_terms(volume_rows, power_rows, sigma2, inputs[0], inputs[1], inputs[2], inputs[3], inputs[4])
        return (running[0] + data_sum, running[1] + weight_sum), evidence

    initial = (jnp.zeros((columns, 2 * FREQ), jnp.float32), jnp.zeros((columns, FREQ), jnp.float32))
    inputs = (particles.reshape(blocks, block_rows, 2, FREQ), defocus.reshape(blocks, block_rows), center.reshape(blocks, block_rows), orient.reshape(blocks, block_rows, CANDS), live_slots.reshape(blocks, block_rows))
    totals, evidence = lax.scan(scan_step, initial, inputs)
    estimate = totals[0].reshape(CLASSES, ORIENTS, 2, FREQ) / (totals[1].reshape(CLASSES, ORIENTS, 1, FREQ) + WIENER_TERM)
    return estimate, evidence.reshape(PARTICLES)
```

```python
import math

import jax
import jax.numpy as jnp
import numpy as np
from jax import lax
from jax.experimental import pallas as pl
from jax.experimental.pallas import tpu as pltpu
from jax.sharding import PartitionSpec as P

FSIDE = 64
BOX = 128
GRID = 9
SHIFTS = 9
ORIENTS = 48
CANDS = 16
SLAB = 32

CTF_GAIN = 400.0
CTF_PHASE = 0.07
WIENER_TERM = 0.002

NX, NY, NL, NH, NZ = 4, 4, 2, 4, 8
BLOCKS = 32
COLS = NH * ORIENTS
PAIR = 2 * SLAB
ROWS = 640
MESH = pl.DeviceIdType.MESH
F32, BF16 = jnp.float32, jnp.bfloat16

SIN_TERMS = (6.2831853025115025, -41.34170040531776, 81.60513138580835, -76.70301535406267,
             42.02592698764344, -14.899846674846755, 3.2381375198594955)
COS_TERMS = (0.9999999890590235, -19.73920449945402, 64.93911745989969, -85.45013953094733,
             60.16763095140483, -25.96759924996967, 6.5286581631738425)

AG_Z = 0
AG_2 = 7
AG_3 = 15
PART = 23
AUX_C = 24
AUX_R = 25
NORM = 26
RS_1 = 27
RS_2 = 39
RS_Z = 51
COPIES = 58


def poly(terms, x):
    total = terms[-1] * x + terms[-2]
    for term in terms[-3::-1]:
        total = total * x + term
    return total


def sin_turns(t):
    return poly(SIN_TERMS, t * t) * t


def cos_turns(t):
    return poly(COS_TERMS, t * t)


def frequency_tables():
    position = np.arange(FSIDE * FSIDE)
    u = position % FSIDE
    v = position // FSIDE - FSIDE // 2
    tables = np.stack(
        [(u * u + v * v) / (BOX * BOX), v, np.cos(2 * np.pi * v / BOX), np.sin(2 * np.pi * v / BOX)]
    )
    lanes = np.zeros((8, 128))
    lanes[0] = u[:128]
    lanes[1] = np.cos(2 * np.pi * u[:128] / BOX)
    lanes[2] = np.sin(2 * np.pi * u[:128] / BOX)
    return (tables.reshape(4, BLOCKS, 128).astype(np.float32), lanes.astype(np.float32))


def kernel(
    part_ref, auxc_ref, auxr_ref, proj_ref, tab_ref, lane_ref, isg_ref,
    est_ref, evid_ref,
    gath, imgs, auxc, auxr, norm, shifted, ctf, corr, power_sum, expo, post,
    send1, recv1, sums1, send2, recv2, sums2, recv3,
    send_sem, recv_sem, local_sem,
):
    dom, cls = lax.axis_index("dom"), lax.axis_index("cls")
    z_lo, x, y = lax.rem(dom, 2), lax.rem(dom // 2, 4), dom // 8
    core, z_hi = lax.rem(cls, 2), cls // 2
    z = z_hi * 2 + z_lo

    def device(yy, xx, zz):
        return ((yy * NX + xx) * 2 + lax.rem(zz, 2), (zz // 2) * 2 + core)

    def ring4(position, step):
        return lax.rem(position + step + 4, 4)

    def along(axis, step):
        if axis == 0:
            return device(y, ring4(x, step), z)
        return device(ring4(y, step), x, z)

    here = (x, y)
    partner = (dom, z_hi * 2 + 1 - core)

    def around(step):
        return lax.rem(z + step + NZ, NZ)

    def copy(index, source, target, to):
        return pltpu.make_async_remote_copy(
            src_ref=source, dst_ref=target, send_sem=send_sem.at[index],
            recv_sem=recv_sem.at[index], device_id=to, device_id_type=MESH,
        )

    pending = []

    def send(index, source, target, to):
        out = copy(index, source, target, to)
        out.start()
        pending.append(out)

    def arrived(index, target):
        copy(index, target, target, partner).wait_recv()

    barrier = pltpu.get_barrier_semaphore()
    friends = [partner]
    friends += [along(axis, step) for axis in (0, 1) for step in (1, -1)]
    friends += [device(y, x, around(step)) for step in range(1, NZ)]
    for friend in friends:
        pl.semaphore_signal(barrier, inc=1, device_id=friend, device_id_type=MESH)

    own = [
        pltpu.make_async_copy(part_ref, imgs.at[core], local_sem.at[0]),
        pltpu.make_async_copy(auxc_ref, auxc.at[core], local_sem.at[1]),
        pltpu.make_async_copy(auxr_ref, auxr.at[core], local_sem.at[2]),
        pltpu.make_async_copy(proj_ref, gath.at[y, x, z_lo, z_hi], local_sem.at[3]),
    ]
    for item in own:
        item.start()
    pl.semaphore_wait(barrier, len(friends))

    mine = gath.at[y, x, z_lo, z_hi]
    for step in range(1, NZ):
        send(AG_Z + step - 1, proj_ref, mine, device(y, x, around(step)))
    send(PART, part_ref, imgs.at[core], partner)
    send(AUX_C, auxc_ref, auxc.at[core], partner)
    send(AUX_R, auxr_ref, auxr.at[core], partner)
    for item in own:
        item.wait()

    u = lane_ref[0:1, :]
    cos_u, sin_u = lane_ref[1:2, :], lane_ref[2:3, :]

    def shift_tile(owner, tile):
        start = tile * 16
        info = auxc[owner, start:start + 16, :]
        gain, t_x, t_y = info[:, 0:1], info[:, 1:2], info[:, 2:3]
        base_turn = u * t_x
        row0 = owner * SLAB + start

        def rows_at(base):
            return pl.ds(pl.multiple_of(base + row0, 16), 16)

        def step(d, carry):
            radius = tab_ref[0, pl.ds(d, 1), :]
            v = tab_ref[1, pl.ds(d, 1), :]
            cos_v = tab_ref[2, pl.ds(d, 1), :]
            sin_v = tab_ref[3, pl.ds(d, 1), :]
            inverse = isg_ref[pl.ds(d, 1), :]
            lanes = pl.ds(pl.multiple_of(d * 128, 128), 128)
            real = imgs[owner, 0, pl.ds(start, 16), lanes].astype(F32)
            imag = imgs[owner, 1, pl.ds(start, 16), lanes].astype(F32)
            angle = gain * radius + CTF_PHASE
            turns = jnp.floor(angle * (0.5 / math.pi) + 0.5)
            rest = (angle - turns * 6.28125) - turns * 0.0019353071795864769
            contrast = -sin_turns(rest * (0.5 / math.pi))
            weight = contrast * inverse
            ctf_weight = (contrast * contrast * inverse).astype(BF16)
            ctf[d, rows_at(0), :] = ctf_weight
            ctf[d, rows_at(PAIR), :] = ctf_weight
            turn = (base_turn + v * t_y) * (1.0 / BOX)
            turn = turn - jnp.floor(turn + 0.5)
            cosine, sine = cos_turns(turn), sin_turns(turn)
            real, imag = real * weight, imag * weight
            mid = (real * cosine - imag * sine, real * sine + imag * cosine)

            def rotations(value, cos_, sin_):
                re, im = value
                re_c, re_s, im_c, im_s = re * cos_, re * sin_, im * cos_, im * sin_
                return ((re_c + im_s, im_c - re_s), value, (re_c - im_s, im_c + re_s))

            for d_y, moved in enumerate(rotations(mid, cos_v, sin_v)):
                for d_x, (re, im) in enumerate(rotations(moved, cos_u, sin_u)):
                    at = rows_at((d_y * 3 + d_x) * PAIR)
                    shifted[d, at, 0:128] = re.astype(BF16)
                    shifted[d, at, 128:256] = im.astype(BF16)
            return carry

        lax.fori_loop(0, BLOCKS, step, 0)

    def zero_step(d, carry):
        shifted[d, SHIFTS * PAIR:, :] = jnp.zeros((ROWS - SHIFTS * PAIR, 256), BF16)
        return carry

    def view(half, stage, position, part=None):
        cut = slice(None) if part is None else pl.ds(2 * part, 2)
        if stage == 0:
            if half == 0:
                return gath.at[y, position, 0, cut]
            return gath.at[position, x, 1, cut]
        if half == 0:
            return gath.at[position, cut, 0]
        return gath.at[cut, position, 1]

    def ring_first(half, stage):
        axis = half if stage == 0 else 1 - half
        base = (AG_2 if stage == 0 else AG_3) + 4 * half
        ref = view(half, stage, here[axis])
        send(base, ref, ref, along(axis, 1))
        send(base + 1, ref, ref, along(axis, -1))

    def ring_second(half, stage):
        axis = half if stage == 0 else 1 - half
        base = (AG_2 if stage == 0 else AG_3) + 4 * half
        left, right = ring4(here[axis], -1), ring4(here[axis], 1)
        arrived(base, view(half, stage, left))
        ref = view(half, stage, left, 0)
        send(base + 2, ref, ref, along(axis, 1))
        arrived(base + 1, view(half, stage, right))
        ref = view(half, stage, right, 1)
        send(base + 3, ref, ref, along(axis, -1))

    def ring_end(half, stage):
        axis = half if stage == 0 else 1 - half
        base = (AG_2 if stage == 0 else AG_3) + 4 * half
        far = ring4(here[axis], 2)
        arrived(base + 2, view(half, stage, far, 0))
        arrived(base + 3, view(half, stage, far, 1))

    shift_tile(core, 0)
    for step in range(1, NZ):
        from_z = around(-step)
        arrived(AG_Z + step - 1, gath.at[y, x, lax.rem(from_z, 2), from_z // 2])
    for half in (0, 1):
        ring_first(half, 0)
    shift_tile(core, 1)
    for half in (0, 1):
        ring_second(half, 0)
    lax.fori_loop(0, BLOCKS, zero_step, 0)
    arrived(PART, imgs.at[1 - core])
    arrived(AUX_C, auxc.at[1 - core])
    arrived(AUX_R, auxr.at[1 - core])
    for half in (0, 1):
        ring_end(half, 0)
        ring_first(half, 1)
    shift_tile(1 - core, 0)
    for half in (0, 1):
        ring_second(half, 1)
    shift_tile(1 - core, 1)
    for half in (0, 1):
        ring_end(half, 1)

    contract_last = (((1,), (1,)), ((), ()))
    contract_plain = (((1,), (0,)), ((), ()))
    corr[...] = jnp.zeros_like(corr)
    power_sum[...] = jnp.zeros_like(power_sum)

    def score_step(group, carry):
        yy, xx = group // 4, lax.rem(group, 4)
        total = power = None
        for low in (0, 1):
            d = group * 2 + low
            volumes = gath[yy, xx, low].reshape(COLS, 256)
            re, im = volumes[:, 0:128].astype(F32), volumes[:, 128:256].astype(F32)
            squared = (re * re + im * im).astype(BF16)
            term = lax.dot_general(shifted[d], volumes, contract_last, preferred_element_type=F32)
            term_p = lax.dot_general(squared, ctf[d], contract_last, preferred_element_type=F32)
            total = term if total is None else total + term
            power = term_p if power is None else power + term_p
        corr[:, 0:COLS] += total
        power_sum[...] += power
        return carry

    lax.fori_loop(0, BLOCKS // 2, score_step, 0)

    info = auxr[0] + auxr[1]
    row = lax.broadcasted_iota(jnp.int32, (ORIENTS, 128), 0).astype(F32)
    allowed = jnp.zeros((ORIENTS, 128), jnp.bool_)
    for j in range(CANDS):
        allowed = allowed | (info[j:j + 1, :] == row)
    allowed = jnp.where(allowed, 1.0, 0.0)
    allowed = jnp.concatenate([allowed] * NH, axis=0) > 0.5
    lower = lax.broadcasted_iota(jnp.int32, (COLS, 128), 1) < PAIR
    live = info[CANDS:CANDS + 1, :]
    least = jnp.float32(-3.0e38)
    highest = jnp.full((1, 128), least, F32)
    for tile in range(5):
        lanes = slice(tile * 128, tile * 128 + 128)
        scores = jnp.transpose(corr[lanes, :])[0:COLS, :] - 0.5 * power_sum[...]
        valid = allowed & lower if tile == 4 else allowed
        scores = jnp.where(valid, scores, least)
        expo[:, lanes] = scores
        highest = jnp.maximum(highest, jnp.max(scores, axis=0, keepdims=True))
    highest = jnp.maximum(highest, pltpu.roll(highest, 64, 1))
    partition = jnp.zeros((1, 128), F32)
    for tile in range(5):
        lanes = slice(tile * 128, tile * 128 + 128)
        valid = allowed & lower if tile == 4 else allowed
        terms = jnp.where(valid, jnp.exp(expo[:, lanes] - highest), 0.0)
        expo[:, lanes] = terms
        partition = partition + jnp.sum(terms, axis=0, keepdims=True)
    partition = partition + pltpu.roll(partition, 64, 1)

    norm[core, 0:1, :] = highest
    norm[core, 1:2, :] = partition
    norm[core, 2:8, :] = jnp.zeros((6, 128), F32)
    send(NORM, norm.at[core], norm.at[core], partner)
    arrived(NORM, norm.at[1 - core])
    other = norm[1 - core]
    peak = jnp.maximum(highest, other[0:1, :])
    mine_scale = jnp.exp(highest - peak)
    whole = partition * mine_scale + other[1:2, :] * jnp.exp(other[0:1, :] - peak)
    evidence = jnp.where(live > 0.5, peak + jnp.log(whole), 0.0)
    evid_ref[...] = jnp.broadcast_to(evidence, evid_ref.shape)
    scale = jnp.where(live > 0.5, mine_scale / whole, 0.0)
    mass = jnp.zeros((COLS, 128), F32)
    for tile in range(5):
        lanes = slice(tile * 128, tile * 128 + 128)
        posterior = (expo[:, lanes] * scale).astype(BF16)
        post[:, lanes] = posterior
        mass = mass + posterior.astype(F32)
    mass = mass + pltpu.roll(mass, 64, 1)
    post[:, 640:768] = jnp.where(lower, mass, 0.0).astype(BF16)

    def project(d):
        data = lax.dot_general(
            post[:, 0:ROWS], shifted[d], contract_plain, preferred_element_type=F32
        )
        weight = lax.dot_general(
            post[:, 640:768], ctf[d], contract_plain, preferred_element_type=F32
        )
        return data, weight

    def block_of(half, position, j):
        if half == 0:
            return (j * NX + position) * 2
        return (position * NX + j) * 2 + 1

    def piece(half, slot, position, first, added=None):
        def step(i, carry):
            data, weight = project(block_of(half, position, first + i))
            if added is not None:
                more = recv1[half, added, i].astype(F32)
                data, weight = data + more[:, 0:256], weight + more[:, 256:384]
            send1[half, slot, i, :, 0:256] = data.astype(BF16)
            send1[half, slot, i, :, 256:384] = weight.astype(BF16)
            return carry

        lax.fori_loop(0, 2, step, 0)
        send(
            RS_1 + 6 * half + slot, send1.at[half, slot], recv1.at[half, slot],
            along(half, 1 if slot % 2 == 0 else -1),
        )

    for half in (0, 1):
        far = ring4(here[half], 2)
        piece(half, 0, far, 0)
        piece(half, 1, far, 2)
    for half in (0, 1):
        piece(half, 2, ring4(here[half], 1), 2)
        piece(half, 3, ring4(here[half], -1), 0)
    for half in (0, 1):
        arrived(RS_1 + 6 * half, recv1.at[half, 0])
        piece(half, 4, ring4(here[half], 1), 0, 0)
        arrived(RS_1 + 6 * half + 1, recv1.at[half, 1])
        piece(half, 5, ring4(here[half], -1), 2, 1)

    for half in (0, 1):

        def own_step(j, carry, half=half):
            data, weight = project(block_of(half, here[half], j))
            sums1[half, j, :, 0:256] = data
            sums1[half, j, :, 256:384] = weight
            return carry

        lax.fori_loop(0, 4, own_step, 0)

    for half in (0, 1):
        for slot in range(2, 6):
            arrived(RS_1 + 6 * half + slot, recv1.at[half, slot])

        def add_step(i, carry, half=half):
            sums1[half, i] += recv1[half, 3, i].astype(F32) + recv1[half, 4, i].astype(F32)
            sums1[half, 2 + i] += recv1[half, 2, i].astype(F32) + recv1[half, 5, i].astype(F32)
            return carry

        lax.fori_loop(0, 2, add_step, 0)

        axis = 1 - half
        at = here[axis]
        edge = COLS // 2

        def relay(slot, position, top, half=half, axis=axis):
            value = sums1[half, position, top * edge:(top + 1) * edge, :]
            send2[half, slot] = value
            send(
                RS_2 + 6 * half + slot, send2.at[half, slot], recv2.at[half, slot],
                along(axis, 1 if slot % 2 == 0 else -1),
            )

        relay(0, ring4(at, 2), 0)
        relay(1, ring4(at, 2), 1)
        relay(2, ring4(at, 1), 1)
        relay(3, ring4(at, -1), 0)

    for half in (0, 1):
        axis = 1 - half
        at = here[axis]

        def relay_end(slot, position, top, added, half=half, axis=axis):
            arrived(RS_2 + 6 * half + added, recv2.at[half, added])
            value = sums1[half, position, top * edge:(top + 1) * edge, :]
            send2[half, slot] = value + recv2[half, added]
            send(
                RS_2 + 6 * half + slot, send2.at[half, slot], recv2.at[half, slot],
                along(axis, 1 if slot % 2 == 0 else -1),
            )

        relay_end(4, ring4(at, 1), 0, 0)
        relay_end(5, ring4(at, -1), 1, 1)

    for half in (0, 1):
        for slot in range(2, 6):
            arrived(RS_2 + 6 * half + slot, recv2.at[half, slot])
        at = here[1 - half]
        top = (
            sums1[half, at, 0:edge, :]
            + recv2[half, 3]
            + recv2[half, 4]
        )
        bottom = (
            sums1[half, at, edge:COLS, :]
            + recv2[half, 2]
            + recv2[half, 5]
        )
        for h in range(NH):
            value = (top if h < 2 else bottom)[(h % 2) * ORIENTS:(h % 2 + 1) * ORIENTS, :]
            sums2[half, h] = value

    for step in range(1, NZ):
        to_z = around(step)
        send(
            RS_Z + step - 1, sums2.at[lax.rem(to_z, 2), to_z // 2], recv3.at[step - 1],
            device(y, x, to_z),
        )
    total = sums2[z_lo, z_hi]
    for step in range(1, NZ):
        arrived(RS_Z + step - 1, recv3.at[step - 1])
        total = total + recv3[step - 1]
    divisor = total[:, 256:384] + WIENER_TERM
    est_ref[:, 0:128] = total[:, 0:128] / divisor
    est_ref[:, 128:256] = total[:, 128:256] / divisor

    for item in pending:
        item.wait_send()


def on_device(particles, defocus, orient, center, live, sigma2, projections):
    core = lax.rem(lax.axis_index("cls"), 2)
    tables, lanes = frequency_tables()
    inner_side = GRID - 2
    base_x = (center % inner_side + 1 - GRID // 2).astype(F32)
    base_y = (center // inner_side + 1 - GRID // 2).astype(F32)
    gain = CTF_GAIN * defocus.astype(F32)
    columns = jnp.zeros((SLAB, 125), F32)
    aux_columns = jnp.concatenate(
        [gain[:, None], base_x[:, None], base_y[:, None], columns], axis=1
    )
    is_live = (jnp.arange(SLAB, dtype=jnp.int32) < live[0]).astype(F32)
    rows = jnp.concatenate(
        [orient.astype(F32).T, is_live[None, :], jnp.zeros((7, SLAB), F32)], axis=0
    )
    nothing = jnp.zeros_like(rows)
    first, second = jnp.where(core == 0, rows, nothing), jnp.where(core == 0, nothing, rows)
    aux_rows = jnp.concatenate([first, second, first, second], axis=1)
    images = particles.transpose(1, 0, 2)
    chunk = projections.reshape(ORIENTS, 256)
    inverse = (1.0 / sigma2).reshape(BLOCKS, 128)
    vmem = pl.BlockSpec(memory_space=pltpu.VMEM)
    estimate, evidence = pl.pallas_call(
        kernel,
        out_shape=(
            jax.ShapeDtypeStruct((ORIENTS, 256), F32),
            jax.ShapeDtypeStruct((8, 128), F32),
        ),
        in_specs=[vmem] * 7,
        out_specs=(vmem, vmem),
        scratch_shapes=[
            pltpu.VMEM((NY, NX, NL, NH, ORIENTS, 256), BF16),
            pltpu.VMEM((2, 2, SLAB, FSIDE * FSIDE), BF16),
            pltpu.VMEM((2, SLAB, 128), F32),
            pltpu.VMEM((2, 24, 128), F32),
            pltpu.VMEM((2, 8, 128), F32),
            pltpu.VMEM((BLOCKS, ROWS, 256), BF16),
            pltpu.VMEM((BLOCKS, 128, 128), BF16),
            pltpu.VMEM((ROWS, 256), F32),
            pltpu.VMEM((COLS, 128), F32),
            pltpu.VMEM((COLS, ROWS), F32),
            pltpu.VMEM((COLS, 768), BF16),
            pltpu.VMEM((2, 6, 2, COLS, 384), BF16),
            pltpu.VMEM((2, 6, 2, COLS, 384), BF16),
            pltpu.VMEM((2, 4, COLS, 384), F32),
            pltpu.VMEM((2, 6, COLS // 2, 384), F32),
            pltpu.VMEM((2, 6, COLS // 2, 384), F32),
            pltpu.VMEM((2, NH, ORIENTS, 384), F32),
            pltpu.VMEM((NZ - 1, ORIENTS, 384), F32),
            pltpu.SemaphoreType.DMA((COPIES,)),
            pltpu.SemaphoreType.DMA((COPIES,)),
            pltpu.SemaphoreType.DMA((4,)),
        ],
        compiler_params=pltpu.CompilerParams(
            collective_id=0, has_side_effects=True, vmem_limit_bytes=50 * 1024 * 1024
        ),
    )(images, aux_columns, aux_rows, chunk, jnp.asarray(tables), jnp.asarray(lanes), inverse)
    evidence = lax.dynamic_slice(evidence, (0, core * SLAB), (1, SLAB)).reshape(SLAB)
    return (estimate.reshape(1, ORIENTS, 2, 128), evidence)


def solution(mesh):
    return jax.shard_map(
        on_device,
        mesh=mesh,
        in_specs=(
            P(("dom", "cls"), None, None),
            P(("dom", "cls")),
            P(("dom", "cls"), None),
            P(("dom", "cls")),
            P(("dom", "cls")),
            P(),
            P("cls", None, None, "dom"),
        ),
        out_specs=(P("cls", None, None, "dom"), P(("dom", "cls"))),
        check_vma=False,
    )
```

```python
import math

import jax
import jax.numpy as jnp
import numpy as np
from jax import lax
from jax.experimental import pallas as pl
from jax.experimental.pallas import tpu as pltpu
from jax.sharding import PartitionSpec as P

FSIDE = 64
BOX = 128
GRID = 9
SHIFTS = 9
ORIENTS = 48
CANDS = 16
SLAB = 32

CTF_GAIN = 400.0
CTF_PHASE = 0.07
WIENER_TERM = 0.002

NX, NY, NL, NH, NZ = 4, 4, 2, 4, 8
BLOCKS = 32
COLS = NH * ORIENTS
PAIR = 2 * SLAB
ROWS = 640
MESH = pl.DeviceIdType.MESH
F32, BF16 = jnp.float32, jnp.bfloat16

SIN_TERMS = (6.2831853025115025, -41.34170040531776, 81.60513138580835, -76.70301535406267,
             42.02592698764344, -14.899846674846755, 3.2381375198594955)
COS_TERMS = (0.9999999890590235, -19.73920449945402, 64.93911745989969, -85.45013953094733,
             60.16763095140483, -25.96759924996967, 6.5286581631738425)

AG_Z = 0
AG_2 = 7
AG_3 = 15
PART, PART_Z, PART_F = 39, 40, 41
AUX_C, AUX_Z, AUX_F, AUX_R = 42, 43, 44, 45
NORM, POST = 46, 47
RS_1 = 48
RS_2 = 60
RS_Z = 72
COPIES = 75


def poly(terms, x):
    total = terms[-1] * x + terms[-2]
    for term in terms[-3::-1]:
        total = total * x + term
    return total


def sin_turns(t):
    return poly(SIN_TERMS, t * t) * t


def cos_turns(t):
    return poly(COS_TERMS, t * t)


def frequency_tables():
    position = np.arange(FSIDE * FSIDE)
    u = position % FSIDE
    v = position // FSIDE - FSIDE // 2
    tables = np.stack(
        [(u * u + v * v) / (BOX * BOX), v, np.cos(2 * np.pi * v / BOX), np.sin(2 * np.pi * v / BOX)]
    )
    lanes = np.zeros((8, 128))
    lanes[0] = u[:128]
    lanes[1] = np.cos(2 * np.pi * u[:128] / BOX)
    lanes[2] = np.sin(2 * np.pi * u[:128] / BOX)
    tables = tables.reshape(4, 16, 2, 128).transpose(0, 2, 1, 3).reshape(4, BLOCKS, 128)
    return (tables.astype(np.float32), lanes.astype(np.float32))


def kernel(
    part_ref, auxc_ref, auxr_ref, proj_ref, tab_ref, lane_ref, isg_ref,
    est_ref, evid_ref,
    gath, imgs, auxc, auxr, norm, shifted, ctf, corr, power_sum, expo, post, post_z,
    acc, send1, recv1, send2, recv2, sums2, recv3,
    send_sem, recv_sem, local_sem,
):
    dom, cls = lax.axis_index("dom"), lax.axis_index("cls")
    z_lo, x, y = lax.rem(dom, 2), lax.rem(dom // 2, 4), dom // 8
    core, z_hi = lax.rem(cls, 2), cls // 2
    z = z_hi * 2 + z_lo

    def device(yy, xx, zz):
        return ((yy * NX + xx) * 2 + lax.rem(zz, 2), (zz // 2) * 2 + core)

    def ring4(position, step):
        return lax.rem(position + step + 4, 4)

    def along(axis, step):
        if axis == 0:
            return device(y, ring4(x, step), z)
        return device(ring4(y, step), x, z)

    here = (x, y)
    partner = (dom, z_hi * 2 + 1 - core)
    beside = device(y, x, z_hi * 2 + 1 - z_lo)

    def around(step):
        return lax.rem(z + step + NZ, NZ)

    def copy(index, source, target, to):
        return pltpu.make_async_remote_copy(
            src_ref=source, dst_ref=target, send_sem=send_sem.at[index],
            recv_sem=recv_sem.at[index], device_id=to, device_id_type=MESH,
        )

    pending = []

    def send(index, source, target, to):
        out = copy(index, source, target, to)
        out.start()
        pending.append(out)

    def arrived(index, target):
        copy(index, target, target, partner).wait_recv()

    barrier = pltpu.get_barrier_semaphore()
    friends = [partner]
    friends += [along(axis, step) for axis in (0, 1) for step in (1, -1)]
    friends += [device(y, x, around(step)) for step in range(1, NZ)]
    for friend in friends:
        pl.semaphore_signal(barrier, inc=1, device_id=friend, device_id_type=MESH)

    own = [
        pltpu.make_async_copy(part_ref, imgs.at[pl.ds(0, 2), core], local_sem.at[0]),
        pltpu.make_async_copy(auxc_ref, auxc.at[0, core], local_sem.at[1]),
        pltpu.make_async_copy(auxr_ref, auxr.at[core], local_sem.at[2]),
        pltpu.make_async_copy(proj_ref, gath.at[y, x, z_lo, z_hi], local_sem.at[3]),
    ]
    for item in own:
        item.start()
    pl.semaphore_wait(barrier, len(friends))

    mine = gath.at[y, x, z_lo, z_hi]
    for step in range(1, NZ):
        send(AG_Z + step - 1, proj_ref, mine, device(y, x, around(step)))
    send(PART, part_ref, imgs.at[pl.ds(0, 2), core], partner)
    send(AUX_C, auxc_ref, auxc.at[0, core], partner)
    send(AUX_R, auxr_ref, auxr.at[core], partner)
    send(PART_Z, part_ref.at[1 - z_lo], imgs.at[2, core], beside)
    send(AUX_Z, auxc_ref, auxc.at[1, core], beside)
    for item in own:
        item.wait()

    u = lane_ref[0:1, :]
    cos_u, sin_u = lane_ref[1:2, :], lane_ref[2:3, :]

    def shift_tile(group, owner, tile):
        start = tile * 16
        info = auxc[0 if group < 2 else 1, owner, start:start + 16, :]
        gain, t_x, t_y = info[:, 0:1], info[:, 1:2], info[:, 2:3]
        base_turn = u * t_x
        row0 = owner * SLAB + start

        def rows_at(base):
            return pl.ds(pl.multiple_of(base + row0, 16), 16)

        def step(at_yx, carry):
            d = (group if group < 2 else z_lo) * 16 + at_yx
            block = group * 16 + at_yx
            radius = tab_ref[0, pl.ds(d, 1), :]
            v = tab_ref[1, pl.ds(d, 1), :]
            cos_v = tab_ref[2, pl.ds(d, 1), :]
            sin_v = tab_ref[3, pl.ds(d, 1), :]
            inverse = isg_ref[pl.ds(d, 1), :]
            lanes = pl.ds(pl.multiple_of(at_yx * 128, 128), 128)
            real = imgs[group, owner, 0, pl.ds(start, 16), lanes].astype(F32)
            imag = imgs[group, owner, 1, pl.ds(start, 16), lanes].astype(F32)
            angle = gain * radius + CTF_PHASE
            turns = jnp.floor(angle * (0.5 / math.pi) + 0.5)
            rest = (angle - turns * 6.28125) - turns * 0.0019353071795864769
            contrast = -sin_turns(rest * (0.5 / math.pi))
            weight = contrast * inverse
            ctf_weight = (contrast * contrast * inverse).astype(BF16)
            ctf[block, rows_at(0), :] = ctf_weight
            ctf[block, rows_at(PAIR), :] = ctf_weight
            turn = (base_turn + v * t_y) * (1.0 / BOX)
            turn = turn - jnp.floor(turn + 0.5)
            cosine, sine = cos_turns(turn), sin_turns(turn)
            real, imag = real * weight, imag * weight
            mid = (real * cosine - imag * sine, real * sine + imag * cosine)

            def rotations(value, cos_, sin_):
                re, im = value
                re_c, re_s, im_c, im_s = re * cos_, re * sin_, im * cos_, im * sin_
                return ((re_c + im_s, im_c - re_s), value, (re_c - im_s, im_c + re_s))

            for d_y, moved in enumerate(rotations(mid, cos_v, sin_v)):
                for d_x, (re, im) in enumerate(rotations(moved, cos_u, sin_u)):
                    at = rows_at((d_y * 3 + d_x) * PAIR)
                    shifted[block, at, 0:128] = re.astype(BF16)
                    shifted[block, at, 128:256] = im.astype(BF16)
            return carry

        lax.fori_loop(0, 16, step, 0)

    def zero_step(block, carry):
        shifted[block, SHIFTS * PAIR:, :] = jnp.zeros((ROWS - SHIFTS * PAIR, 256), BF16)
        return carry

    def view(half, position, part=None):
        cut = slice(None) if part is None else pl.ds(2 * part, 2)
        if half == 0:
            return gath.at[y, position, 0, cut]
        return gath.at[position, x, 1, cut]

    def view_piece(half, piece, position):
        if half == 0:
            return gath.at[position, ring4(x, piece), 0]
        return gath.at[ring4(y, piece), position, 1]

    def ring_first(half):
        ref = view(half, here[half])
        send(AG_2 + 4 * half, ref, ref, along(half, 1))
        send(AG_2 + 4 * half + 1, ref, ref, along(half, -1))

    def ring_second(half):
        base = AG_2 + 4 * half
        left, right = ring4(here[half], -1), ring4(here[half], 1)
        arrived(base, view(half, left))
        ref = view(half, left, 0)
        send(base + 2, ref, ref, along(half, 1))
        arrived(base + 1, view(half, right))
        ref = view(half, right, 1)
        send(base + 3, ref, ref, along(half, -1))

    def ring_end(half):
        far = ring4(here[half], 2)
        arrived(AG_2 + 4 * half + 2, view(half, far, 0))
        arrived(AG_2 + 4 * half + 3, view(half, far, 1))

    def piece_first(half, piece):
        axis = 1 - half
        base = AG_3 + 12 * half + 3 * piece
        ref = view_piece(half, piece, here[axis])
        send(base, ref, ref, along(axis, 1))
        send(base + 1, ref, ref, along(axis, -1))

    def piece_second(half, piece):
        axis = 1 - half
        base = AG_3 + 12 * half + 3 * piece
        left = view_piece(half, piece, ring4(here[axis], -1))
        right = view_piece(half, piece, ring4(here[axis], 1))
        if piece % 2 == 0:
            arrived(base, left)
            send(base + 2, left, left, along(axis, 1))
            arrived(base + 1, right)
        else:
            arrived(base + 1, right)
            send(base + 2, right, right, along(axis, -1))
            arrived(base, left)

    def piece_end(half, piece):
        axis = 1 - half
        far = view_piece(half, piece, ring4(here[axis], 2))
        arrived(AG_3 + 12 * half + 3 * piece + 2, far)

    shift_tile(0, core, 0)
    shift_tile(1, core, 0)
    for step in range(1, NZ):
        from_z = around(-step)
        arrived(AG_Z + step - 1, gath.at[y, x, lax.rem(from_z, 2), from_z // 2])
    for half in (0, 1):
        ring_first(half)
    for half in (0, 1):
        piece_first(half, 0)
    shift_tile(0, core, 1)
    for half in (0, 1):
        ring_second(half)
    for half in (0, 1):
        piece_first(half, 1)
        piece_first(half, 3)
    shift_tile(1, core, 1)
    for half in (0, 1):
        ring_end(half)
        piece_first(half, 2)
        piece_second(half, 0)
    arrived(PART_Z, imgs.at[2, core])
    send(PART_F, imgs.at[2, core], imgs.at[2, core], partner)
    arrived(AUX_Z, auxc.at[1, core])
    send(AUX_F, auxc.at[1, core], auxc.at[1, core], partner)
    arrived(PART, imgs.at[pl.ds(0, 2), 1 - core])
    arrived(AUX_C, auxc.at[0, 1 - core])
    arrived(AUX_R, auxr.at[1 - core])
    shift_tile(0, 1 - core, 0)
    shift_tile(1, 1 - core, 0)
    for half in (0, 1):
        piece_second(half, 1)
        piece_second(half, 3)
    shift_tile(0, 1 - core, 1)
    shift_tile(1, 1 - core, 1)
    lax.fori_loop(0, 48, zero_step, 0)
    for half in (0, 1):
        piece_second(half, 2)

    contract_last = (((1,), (1,)), ((), ()))
    contract_plain = (((1,), (0,)), ((), ()))
    corr[...] = jnp.zeros_like(corr)
    power_sum[...] = jnp.zeros_like(power_sum)

    def score_line(half, position):
        def step(i, carry):
            total = power = None
            for k in (0, 1):
                j = i * 2 + k
                yy, xx = (position, j) if half == 0 else (j, position)
                block = half * 16 + yy * 4 + xx
                volumes = gath[yy, xx, half].reshape(COLS, 256)
                re, im = volumes[:, 0:128].astype(F32), volumes[:, 128:256].astype(F32)
                squared = (re * re + im * im).astype(BF16)
                term = lax.dot_general(
                    shifted[block], volumes, contract_last, preferred_element_type=F32
                )
                term_p = lax.dot_general(
                    squared, ctf[block], contract_last, preferred_element_type=F32
                )
                total = term if total is None else total + term
                power = term_p if power is None else power + term_p
            corr[:, 0:COLS] += total
            power_sum[...] += power
            return carry

        lax.fori_loop(0, 2, step, 0)

    for half in (0, 1):
        for step in (0, 1, -1):
            score_line(half, ring4(here[1 - half], step))
    shift_tile(2, core, 0)
    shift_tile(2, core, 1)
    for half in (0, 1):
        for piece in range(4):
            piece_end(half, piece)
        score_line(half, ring4(here[1 - half], 2))

    info = auxr[0] + auxr[1]
    row = lax.broadcasted_iota(jnp.int32, (ORIENTS, 128), 0).astype(F32)
    allowed = jnp.zeros((ORIENTS, 128), jnp.bool_)
    for j in range(CANDS):
        allowed = allowed | (info[j:j + 1, :] == row)
    allowed = jnp.where(allowed, 1.0, 0.0)
    allowed = jnp.concatenate([allowed] * NH, axis=0) > 0.5
    lower = lax.broadcasted_iota(jnp.int32, (COLS, 128), 1) < PAIR
    live = info[CANDS:CANDS + 1, :]
    least = jnp.float32(-3.0e38)
    highest = jnp.full((1, 128), least, F32)
    for tile in range(5):
        lanes = slice(tile * 128, tile * 128 + 128)
        scores = jnp.transpose(corr[lanes, :])[0:COLS, :] - 0.5 * power_sum[...]
        valid = allowed & lower if tile == 4 else allowed
        scores = jnp.where(valid, scores, least)
        expo[:, lanes] = scores
        highest = jnp.maximum(highest, jnp.max(scores, axis=0, keepdims=True))
    highest = jnp.maximum(highest, pltpu.roll(highest, 64, 1))
    partition = jnp.zeros((1, 128), F32)
    for tile in range(5):
        lanes = slice(tile * 128, tile * 128 + 128)
        valid = allowed & lower if tile == 4 else allowed
        terms = jnp.where(valid, jnp.exp(expo[:, lanes] - highest), 0.0)
        expo[:, lanes] = terms
        partition = partition + jnp.sum(terms, axis=0, keepdims=True)
    partition = partition + pltpu.roll(partition, 64, 1)

    norm[core, 0:1, :] = highest
    norm[core, 1:2, :] = partition
    norm[core, 2:8, :] = jnp.zeros((6, 128), F32)
    send(NORM, norm.at[core], norm.at[core], partner)
    arrived(NORM, norm.at[1 - core])
    other = norm[1 - core]
    peak = jnp.maximum(highest, other[0:1, :])
    mine_scale = jnp.exp(highest - peak)
    whole = partition * mine_scale + other[1:2, :] * jnp.exp(other[0:1, :] - peak)
    scale = jnp.where(live > 0.5, mine_scale / whole, 0.0)
    mass = jnp.zeros((COLS, 128), F32)
    for tile in range(5):
        lanes = slice(tile * 128, tile * 128 + 128)
        posterior = (expo[:, lanes] * scale).astype(BF16)
        post[:, lanes] = posterior
        mass = mass + posterior.astype(F32)
    mass = mass + pltpu.roll(mass, 64, 1)
    post[:, 640:768] = jnp.where(lower, mass, 0.0).astype(BF16)
    send(POST, post, post_z, beside)
    evidence = jnp.where(live > 0.5, peak + jnp.log(whole), 0.0)
    evid_ref[...] = jnp.broadcast_to(evidence, evid_ref.shape)

    def project(weights, block):
        data = lax.dot_general(
            weights[:, 0:ROWS], shifted[block], contract_plain, preferred_element_type=F32
        )
        weight = lax.dot_general(
            weights[:, 640:768], ctf[block], contract_plain, preferred_element_type=F32
        )
        return data, weight

    def place(r):
        return ring4(y, r // 4) * 4 + ring4(x, lax.rem(r, 4))

    def own_step(r, carry):
        data, weight = project(post, z_lo * 16 + place(r))
        acc[r, :, 0:256] = data
        acc[r, :, 256:384] = weight
        return carry

    def next_step(r):
        data, weight = project(post_z, 32 + place(r))
        acc[r, :, 0:256] += data
        acc[r, :, 256:384] += weight

    lax.fori_loop(0, 16, own_step, 0)
    arrived(PART_F, imgs.at[2, 1 - core])
    arrived(AUX_F, auxc.at[1, 1 - core])
    shift_tile(2, 1 - core, 0)
    shift_tile(2, 1 - core, 1)
    arrived(POST, post_z)

    edge = COLS // 2

    def piece(half, slot, target, first, added=None):
        rows = slice(half * edge, half * edge + edge)

        def step(i, carry):
            other = first + i
            value = acc[other * 4 + target if half == 0 else target * 4 + other, rows, :]
            if added is not None:
                value = value + recv1[half, added, i].astype(F32)
            send1[half, slot, i] = value.astype(BF16)
            return carry

        lax.fori_loop(0, 2, step, 0)
        send(
            RS_1 + 6 * half + slot, send1.at[half, slot], recv1.at[half, slot],
            along(half, 1 if slot % 2 == 0 else -1),
        )

    def loop(count, index):
        def step(k, carry):
            next_step(index(k))
            return carry

        lax.fori_loop(0, count, step, 0)

    loop(4, lambda k: k * 4 + 2)
    piece(0, 0, 2, 0)
    piece(0, 1, 2, 2)
    loop(3, lambda k: 8 + k + k // 2)
    piece(1, 0, 2, 0)
    piece(1, 1, 2, 2)
    loop(9, lambda k: (k // 3 + k // 6) * 4 + lax.rem(k, 3) + lax.rem(k, 3) // 2)
    for half in (0, 1):
        piece(half, 2, 1, 2)
        piece(half, 3, 3, 0)
    for half in (0, 1):
        arrived(RS_1 + 6 * half, recv1.at[half, 0])
        piece(half, 4, 1, 0, 0)
        arrived(RS_1 + 6 * half + 1, recv1.at[half, 1])
        piece(half, 5, 3, 2, 1)

    def relay_rows(half, top):
        start = half * edge + top * ORIENTS
        return slice(start, start + ORIENTS)

    def relay(half, slot, distance, top, added=None):
        r = distance * 4 if half == 0 else distance
        value = acc[r, relay_rows(half, top), :]
        if added is not None:
            arrived(RS_2 + 6 * half + added, recv2.at[half, added])
            value = value + recv2[half, added]
        send2[half, slot] = value
        send(
            RS_2 + 6 * half + slot, send2.at[half, slot], recv2.at[half, slot],
            along(1 - half, 1 if slot % 2 == 0 else -1),
        )

    for half in (0, 1):
        rows = slice(half * edge, half * edge + edge)
        for slot in range(2, 6):
            arrived(RS_1 + 6 * half + slot, recv1.at[half, slot])
        for other in (2, 1, 3, 0):
            r = other * 4 if half == 0 else other
            i = other % 2
            near, far = (3, 4) if other < 2 else (2, 5)
            acc[r, rows, :] += recv1[half, near, i].astype(F32) + recv1[half, far, i].astype(F32)
        relay(half, 0, 2, 0)
        relay(half, 1, 2, 1)
        relay(half, 2, 1, 1)
        relay(half, 3, 3, 0)
    for half in (0, 1):
        relay(half, 4, 1, 0, 0)
        relay(half, 5, 3, 1, 1)

    for half in (0, 1):
        for slot in range(2, 6):
            arrived(RS_2 + 6 * half + slot, recv2.at[half, slot])
        sums2[half * 2] = acc[0, relay_rows(half, 0), :] + recv2[half, 3] + recv2[half, 4]
        sums2[half * 2 + 1] = acc[0, relay_rows(half, 1), :] + recv2[half, 2] + recv2[half, 5]

    for step in range(1, NH):
        to = ring4(z_hi, step)
        send(RS_Z + step - 1, sums2.at[to], recv3.at[step - 1], device(y, x, to * 2 + z_lo))
    total = sums2[z_hi]
    for step in range(1, NH):
        arrived(RS_Z + step - 1, recv3.at[step - 1])
        total = total + recv3[step - 1]
    divisor = total[:, 256:384] + WIENER_TERM
    est_ref[:, 0:128] = total[:, 0:128] / divisor
    est_ref[:, 128:256] = total[:, 128:256] / divisor

    for item in pending:
        item.wait_send()


def on_device(particles, defocus, orient, center, live, sigma2, projections):
    core = lax.rem(lax.axis_index("cls"), 2)
    tables, lanes = frequency_tables()
    inner_side = GRID - 2
    base_x = (center % inner_side + 1 - GRID // 2).astype(F32)
    base_y = (center // inner_side + 1 - GRID // 2).astype(F32)
    gain = CTF_GAIN * defocus.astype(F32)
    columns = jnp.zeros((SLAB, 125), F32)
    aux_columns = jnp.concatenate(
        [gain[:, None], base_x[:, None], base_y[:, None], columns], axis=1
    )
    is_live = (jnp.arange(SLAB, dtype=jnp.int32) < live[0]).astype(F32)
    rows = jnp.concatenate(
        [orient.astype(F32).T, is_live[None, :], jnp.zeros((7, SLAB), F32)], axis=0
    )
    nothing = jnp.zeros_like(rows)
    first, second = jnp.where(core == 0, rows, nothing), jnp.where(core == 0, nothing, rows)
    aux_rows = jnp.concatenate([first, second, first, second], axis=1)
    images = particles.reshape(SLAB, 2, 16, 2, 128).transpose(3, 1, 0, 2, 4).reshape(2, 2, SLAB, 2048)
    chunk = projections.reshape(ORIENTS, 256)
    inverse = (1.0 / sigma2).reshape(16, 2, 128).transpose(1, 0, 2).reshape(BLOCKS, 128)
    vmem = pl.BlockSpec(memory_space=pltpu.VMEM)
    estimate, evidence = pl.pallas_call(
        kernel,
        out_shape=(
            jax.ShapeDtypeStruct((ORIENTS, 256), F32),
            jax.ShapeDtypeStruct((8, 128), F32),
        ),
        in_specs=[vmem] * 7,
        out_specs=(vmem, vmem),
        scratch_shapes=[
            pltpu.VMEM((NY, NX, NL, NH, ORIENTS, 256), BF16),
            pltpu.VMEM((3, 2, 2, SLAB, 2048), BF16),
            pltpu.VMEM((2, 2, SLAB, 128), F32),
            pltpu.VMEM((2, 24, 128), F32),
            pltpu.VMEM((2, 8, 128), F32),
            pltpu.VMEM((48, ROWS, 256), BF16),
            pltpu.VMEM((48, 128, 128), BF16),
            pltpu.VMEM((ROWS, 256), F32),
            pltpu.VMEM((COLS, 128), F32),
            pltpu.VMEM((COLS, ROWS), F32),
            pltpu.VMEM((COLS, 768), BF16),
            pltpu.VMEM((COLS, 768), BF16),
            pltpu.VMEM((16, COLS, 384), F32),
            pltpu.VMEM((2, 6, 2, COLS // 2, 384), BF16),
            pltpu.VMEM((2, 6, 2, COLS // 2, 384), BF16),
            pltpu.VMEM((2, 6, ORIENTS, 384), F32),
            pltpu.VMEM((2, 6, ORIENTS, 384), F32),
            pltpu.VMEM((NH, ORIENTS, 384), F32),
            pltpu.VMEM((NH - 1, ORIENTS, 384), F32),
            pltpu.SemaphoreType.DMA((COPIES,)),
            pltpu.SemaphoreType.DMA((COPIES,)),
            pltpu.SemaphoreType.DMA((4,)),
        ],
        compiler_params=pltpu.CompilerParams(
            collective_id=0, has_side_effects=True, vmem_limit_bytes=50 * 1024 * 1024
        ),
    )(images, aux_columns, aux_rows, chunk, jnp.asarray(tables), jnp.asarray(lanes), inverse)
    evidence = lax.dynamic_slice(evidence, (0, core * SLAB), (1, SLAB)).reshape(SLAB)
    return (estimate.reshape(1, ORIENTS, 2, 128), evidence)


def solution(mesh):
    return jax.shard_map(
        on_device,
        mesh=mesh,
        in_specs=(
            P(("dom", "cls"), None, None),
            P(("dom", "cls")),
            P(("dom", "cls"), None),
            P(("dom", "cls")),
            P(("dom", "cls")),
            P(),
            P("cls", None, None, "dom"),
        ),
        out_specs=(P("cls", None, None, "dom"), P(("dom", "cls"))),
        check_vma=False,
    )
```

```python
import math

import jax
import jax.numpy as jnp
from jax import lax
from jax.experimental import pallas as pl
from jax.experimental.pallas import tpu as pltpu
from jax.sharding import PartitionSpec as P

FSIDE = 64
BOX = 128
GRID = 9
SHIFTS = 9
ORIENTS = 48
CANDS = 16
SLAB = 32

CTF_GAIN = 400.0
CTF_PHASE = 0.07
WIENER_TERM = 0.002

NX, NY, NL, NH, NZ = 4, 4, 2, 4, 8
BLOCKS = 32
COLS = NH * ORIENTS
PAIR = 2 * SLAB
ROWS = 640
MESH = pl.DeviceIdType.MESH
F32, BF16 = jnp.float32, jnp.bfloat16

SIN_TERMS = (6.2831853025115025, -41.34170040531776, 81.60513138580835, -76.70301535406267,
             42.02592698764344, -14.899846674846755, 3.2381375198594955)
COS_TERMS = (0.9999999890590235, -19.73920449945402, 64.93911745989969, -85.45013953094733,
             60.16763095140483, -25.96759924996967, 6.5286581631738425)

AG_Z = 0
AG_2 = 7
AG_3 = 15
PART, PART_Z, PART_F = 39, 40, 41
AUX_C, AUX_Z, AUX_F, AUX_R = 42, 43, 44, 45
NORM, POST = 46, 47
RS_1 = 48
RS_2 = 60
RS_Z = 72
COPIES = 78


def poly(terms, x):
    total = terms[-1] * x + terms[-2]
    for term in terms[-3::-1]:
        total = total * x + term
    return total


def sin_turns(t):
    return poly(SIN_TERMS, t * t) * t


def cos_turns(t):
    return poly(COS_TERMS, t * t)


def kernel(
    part_ref, orient_ref, center_ref, defocus_ref, live_ref, sigma_ref, proj_ref,
    est_ref, evid_ref,
    gath, imgs, auxc, auxr, wide, tables, norm, shifted, ctf, corr, power_sum, expo, post, post_z,
    acc, send1, recv1, send2, recv2, sums2, send3, recv3,
    send_sem, recv_sem, local_sem,
):
    dom, cls = lax.axis_index("dom"), lax.axis_index("cls")
    z_lo, x, y = lax.rem(dom, 2), lax.rem(dom // 2, 4), dom // 8
    core, z_hi = lax.rem(cls, 2), cls // 2
    z = z_hi * 2 + z_lo

    def device(yy, xx, zz):
        return ((yy * NX + xx) * 2 + lax.rem(zz, 2), (zz // 2) * 2 + core)

    def ring4(position, step):
        return lax.rem(position + step + 4, 4)

    def along(axis, step):
        if axis == 0:
            return device(y, ring4(x, step), z)
        return device(ring4(y, step), x, z)

    here = (x, y)
    partner = (dom, z_hi * 2 + 1 - core)
    beside = device(y, x, z_hi * 2 + 1 - z_lo)

    def around(step):
        return lax.rem(z + step + NZ, NZ)

    def copy(index, source, target, to):
        return pltpu.make_async_remote_copy(
            src_ref=source, dst_ref=target, send_sem=send_sem.at[index],
            recv_sem=recv_sem.at[index], device_id=to, device_id_type=MESH,
        )

    pending = []

    def send(index, source, target, to):
        out = copy(index, source, target, to)
        out.start()
        pending.append(out)

    def arrived(index, target):
        copy(index, target, target, partner).wait_recv()

    barrier = pltpu.get_barrier_semaphore()
    friends = [partner]
    friends += [along(axis, step) for axis in (0, 1) for step in (1, -1)]
    friends += [device(y, x, around(step)) for step in range(1, NZ)]
    for friend in friends:
        pl.semaphore_signal(barrier, inc=1, device_id=friend, device_id_type=MESH)

    own = [
        pltpu.make_async_copy(part_ref, imgs.at[pl.ds(0, 2), core], local_sem.at[0]),
        pltpu.make_async_copy(proj_ref, gath.at[y, x, z_lo, z_hi], local_sem.at[1]),
    ]
    for item in own:
        item.start()
    pl.semaphore_wait(barrier, len(friends))

    mine = gath.at[y, x, z_lo, z_hi]
    for step in range(1, NZ):
        send(AG_Z + step - 1, proj_ref, mine, device(y, x, around(step)))
    send(PART, part_ref, imgs.at[pl.ds(0, 2), core], partner)

    center = center_ref[...].astype(F32)
    center_y = jnp.floor((center + 0.5) * (1.0 / (GRID - 2)))
    center_x = center - center_y * (GRID - 2)
    slot = lax.broadcasted_iota(jnp.int32, (1, SLAB), 1)
    wide[...] = jnp.zeros_like(wide)
    wide[0:CANDS, 0:SLAB] = orient_ref[...].astype(F32)
    wide[16:17, 0:SLAB] = jnp.where(slot < live_ref[...], 1.0, 0.0)
    wide[17:18, 0:SLAB] = CTF_GAIN * defocus_ref[...].astype(F32)
    wide[18:19, 0:SLAB] = center_x + (1 - GRID // 2)
    wide[19:20, 0:SLAB] = center_y + (1 - GRID // 2)
    placed = pltpu.roll(wide[0:24, :], core * SLAB, 1)
    auxr[core] = placed + pltpu.roll(placed, 64, 1)
    auxc[0, core] = jnp.transpose(wide[...])[0:SLAB, :]
    send(AUX_C, auxc.at[0, core], auxc.at[0, core], partner)
    send(AUX_R, auxr.at[core], auxr.at[core], partner)
    send(AUX_Z, auxc.at[0, core], auxc.at[1, core], beside)

    block_row = lax.broadcasted_iota(jnp.int32, (BLOCKS, 128), 0)
    lane = lax.broadcasted_iota(jnp.int32, (BLOCKS, 128), 1)
    v_all = (block_row * 2 + lane // FSIDE - FSIDE // 2).astype(F32)
    u_all = lax.rem(lane, FSIDE).astype(F32)
    tables[0] = (u_all * u_all + v_all * v_all) * (1.0 / (BOX * BOX))
    tables[1] = v_all
    tables[2] = cos_turns(v_all * (1.0 / BOX))
    tables[3] = sin_turns(v_all * (1.0 / BOX))
    tables[4] = 1.0 / sigma_ref[...]
    u = u_all[0:1, :]
    cos_u, sin_u = cos_turns(u * (1.0 / BOX)), sin_turns(u * (1.0 / BOX))
    for item in own:
        item.wait()

    def shift_tile(group, owner, tile):
        start = tile * 16
        info = auxc[0 if group < 2 else 1, owner, start:start + 16, :]
        gain, t_x, t_y = info[:, 17:18], info[:, 18:19], info[:, 19:20]
        base_turn = u * t_x
        row0 = owner * SLAB + start

        def rows_at(base):
            return pl.ds(pl.multiple_of(base + row0, 16), 16)

        def step(at_yx, carry):
            d = at_yx * 2 + (group if group < 2 else z_lo)
            block = group * 16 + at_yx
            radius = tables[0, pl.ds(d, 1), :]
            v = tables[1, pl.ds(d, 1), :]
            cos_v = tables[2, pl.ds(d, 1), :]
            sin_v = tables[3, pl.ds(d, 1), :]
            inverse = tables[4, pl.ds(d, 1), :]
            lanes = pl.ds(pl.multiple_of(at_yx * 128, 128), 128)
            real = imgs[group, owner, 0, pl.ds(start, 16), lanes].astype(F32)
            imag = imgs[group, owner, 1, pl.ds(start, 16), lanes].astype(F32)
            angle = gain * radius + CTF_PHASE
            turns = jnp.floor(angle * (0.5 / math.pi) + 0.5)
            rest = (angle - turns * 6.28125) - turns * 0.0019353071795864769
            contrast = -sin_turns(rest * (0.5 / math.pi))
            weight = contrast * inverse
            ctf_weight = (contrast * contrast * inverse).astype(BF16)
            ctf[block, rows_at(PAIR), :] = ctf_weight
            turn = (base_turn + v * t_y) * (1.0 / BOX)
            turn = turn - jnp.floor(turn + 0.5)
            cosine, sine = cos_turns(turn), sin_turns(turn)
            real, imag = real * weight, imag * weight
            mid = (real * cosine - imag * sine, real * sine + imag * cosine)

            def rotations(value, cos_, sin_):
                re, im = value
                re_c, re_s, im_c, im_s = re * cos_, re * sin_, im * cos_, im * sin_
                return ((re_c + im_s, im_c - re_s), value, (re_c - im_s, im_c + re_s))

            for d_y, moved in enumerate(rotations(mid, cos_v, sin_v)):
                for d_x, (re, im) in enumerate(rotations(moved, cos_u, sin_u)):
                    at = rows_at((d_y * 3 + d_x) * PAIR)
                    shifted[block, at, 0:128] = re.astype(BF16)
                    shifted[block, at, 128:256] = im.astype(BF16)
            return carry

        lax.fori_loop(0, 16, step, 0)

    def zero_step(block, carry):
        shifted[block, SHIFTS * PAIR:, :] = jnp.zeros((ROWS - SHIFTS * PAIR, 256), BF16)
        ctf[block, 0:PAIR, :] = jnp.zeros((PAIR, 128), BF16)
        return carry

    def view(half, position, part=None):
        cut = slice(None) if part is None else pl.ds(2 * part, 2)
        if half == 0:
            return gath.at[y, position, 0, cut]
        return gath.at[position, x, 1, cut]

    def view_piece(half, piece, position):
        if half == 0:
            return gath.at[position, ring4(x, piece), 0]
        return gath.at[ring4(y, piece), position, 1]

    def ring_first(half):
        ref = view(half, here[half])
        send(AG_2 + 4 * half, ref, ref, along(half, 1))
        send(AG_2 + 4 * half + 1, ref, ref, along(half, -1))

    def ring_second(half):
        base = AG_2 + 4 * half
        left, right = ring4(here[half], -1), ring4(here[half], 1)
        arrived(base, view(half, left))
        ref = view(half, left, 0)
        send(base + 2, ref, ref, along(half, 1))
        arrived(base + 1, view(half, right))
        ref = view(half, right, 1)
        send(base + 3, ref, ref, along(half, -1))

    def ring_end(half):
        far = ring4(here[half], 2)
        arrived(AG_2 + 4 * half + 2, view(half, far, 0))
        arrived(AG_2 + 4 * half + 3, view(half, far, 1))

    def piece_first(half, piece):
        axis = 1 - half
        base = AG_3 + 12 * half + 3 * piece
        ref = view_piece(half, piece, here[axis])
        send(base, ref, ref, along(axis, 1))
        send(base + 1, ref, ref, along(axis, -1))

    def piece_second(half, piece):
        axis = 1 - half
        base = AG_3 + 12 * half + 3 * piece
        left = view_piece(half, piece, ring4(here[axis], -1))
        right = view_piece(half, piece, ring4(here[axis], 1))
        if piece % 2 == 0:
            arrived(base, left)
            send(base + 2, left, left, along(axis, 1))
            arrived(base + 1, right)
        else:
            arrived(base + 1, right)
            send(base + 2, right, right, along(axis, -1))
            arrived(base, left)

    def piece_end(half, piece):
        axis = 1 - half
        far = view_piece(half, piece, ring4(here[axis], 2))
        arrived(AG_3 + 12 * half + 3 * piece + 2, far)

    shift_tile(0, core, 0)
    shift_tile(1, core, 0)
    for step in range(1, NZ):
        from_z = around(-step)
        arrived(AG_Z + step - 1, gath.at[y, x, lax.rem(from_z, 2), from_z // 2])
    for half in (0, 1):
        ring_first(half)
    for half in (0, 1):
        piece_first(half, 0)
    send(PART_Z, part_ref.at[1 - z_lo], imgs.at[2, core], beside)
    shift_tile(0, core, 1)
    for half in (0, 1):
        ring_second(half)
    for half in (0, 1):
        piece_first(half, 1)
        piece_first(half, 3)
    shift_tile(1, core, 1)
    for half in (0, 1):
        ring_end(half)
        piece_first(half, 2)
    for half in (0, 1):
        piece_second(half, 0)
    arrived(PART, imgs.at[pl.ds(0, 2), 1 - core])
    arrived(AUX_C, auxc.at[0, 1 - core])
    shift_tile(0, 1 - core, 0)
    shift_tile(1, 1 - core, 0)
    arrived(PART_Z, imgs.at[2, core])
    send(PART_F, imgs.at[2, core], imgs.at[2, core], partner)
    arrived(AUX_Z, auxc.at[1, core])
    send(AUX_F, auxc.at[1, core], auxc.at[1, core], partner)
    for half in (0, 1):
        piece_second(half, 1)
        piece_second(half, 3)
    shift_tile(0, 1 - core, 1)
    shift_tile(1, 1 - core, 1)
    for half in (0, 1):
        piece_second(half, 2)
    lax.fori_loop(0, 48, zero_step, 0)

    contract_last = (((1,), (1,)), ((), ()))
    contract_plain = (((1,), (0,)), ((), ()))
    corr[...] = jnp.zeros_like(corr)
    power_sum[...] = jnp.zeros_like(power_sum)

    def score_line(half, position):
        def step(i, carry):
            total = power = None
            for k in (0, 1):
                j = i * 2 + k
                yy, xx = (position, j) if half == 0 else (j, position)
                block = half * 16 + yy * 4 + xx
                volumes = gath[yy, xx, half].reshape(COLS, 256)
                re, im = volumes[:, 0:128].astype(F32), volumes[:, 128:256].astype(F32)
                squared = (re * re + im * im).astype(BF16)
                term = lax.dot_general(
                    shifted[block], volumes, contract_last, preferred_element_type=F32
                )
                term_p = lax.dot_general(
                    squared, ctf[block], contract_last, preferred_element_type=F32
                )
                total = term if total is None else total + term
                power = term_p if power is None else power + term_p
            corr[:, 0:COLS] += total
            power_sum[...] += power
            return carry

        lax.fori_loop(0, 2, step, 0)

    for half in (0, 1):
        score_line(half, here[1 - half])
    shift_tile(2, core, 0)
    shift_tile(2, core, 1)
    for half in (0, 1):
        score_line(half, ring4(here[1 - half], 1))
        score_line(half, ring4(here[1 - half], -1))
    arrived(PART_F, imgs.at[2, 1 - core])
    arrived(AUX_F, auxc.at[1, 1 - core])
    shift_tile(2, 1 - core, 0)
    shift_tile(2, 1 - core, 1)
    for half in (0, 1):
        for piece in range(4):
            piece_end(half, piece)
        score_line(half, ring4(here[1 - half], 2))

    arrived(AUX_R, auxr.at[1 - core])
    info = auxr[0] + auxr[1]
    row = lax.broadcasted_iota(jnp.int32, (ORIENTS, 128), 0).astype(F32)
    allowed = jnp.zeros((ORIENTS, 128), jnp.bool_)
    for j in range(CANDS):
        allowed = allowed | (info[j:j + 1, :] == row)
    allowed = jnp.where(allowed, 1.0, 0.0)
    allowed = jnp.concatenate([allowed] * NH, axis=0) > 0.5
    lower = lax.broadcasted_iota(jnp.int32, (COLS, 128), 1) < PAIR
    live = info[CANDS:CANDS + 1, :]
    least = jnp.float32(-3.0e38)
    highest = jnp.full((1, 128), least, F32)
    power_term = power_sum[...] + pltpu.roll(power_sum[...], 64, 1)
    for tile in range(5):
        lanes = slice(tile * 128, tile * 128 + 128)
        scores = jnp.transpose(corr[lanes, :])[0:COLS, :] - 0.5 * power_term
        valid = allowed & lower if tile == 4 else allowed
        scores = jnp.where(valid, scores, least)
        expo[:, lanes] = scores
        highest = jnp.maximum(highest, jnp.max(scores, axis=0, keepdims=True))
    highest = jnp.maximum(highest, pltpu.roll(highest, 64, 1))
    partition = jnp.zeros((1, 128), F32)
    for tile in range(5):
        lanes = slice(tile * 128, tile * 128 + 128)
        valid = allowed & lower if tile == 4 else allowed
        terms = jnp.where(valid, jnp.exp(expo[:, lanes] - highest), 0.0)
        expo[:, lanes] = terms
        partition = partition + jnp.sum(terms, axis=0, keepdims=True)
    partition = partition + pltpu.roll(partition, 64, 1)

    norm[core, 0:1, :] = highest
    norm[core, 1:2, :] = partition
    norm[core, 2:8, :] = jnp.zeros((6, 128), F32)
    send(NORM, norm.at[core], norm.at[core], partner)
    arrived(NORM, norm.at[1 - core])
    other = norm[1 - core]
    peak = jnp.maximum(highest, other[0:1, :])
    mine_scale = jnp.exp(highest - peak)
    whole = partition * mine_scale + other[1:2, :] * jnp.exp(other[0:1, :] - peak)
    scale = jnp.where(live > 0.5, mine_scale / whole, 0.0)
    mass = jnp.zeros((COLS, 128), F32)
    for tile in range(5):
        lanes = slice(tile * 128, tile * 128 + 128)
        posterior = (expo[:, lanes] * scale).astype(BF16).astype(F32)
        mass = mass + posterior
        if tile == 4:
            mass = mass + pltpu.roll(mass, 64, 1)
            posterior = jnp.where(lower, posterior, mass)
        post[:, lanes] = posterior.astype(BF16)
    send(POST, post, post_z, beside)
    evidence = jnp.where(live > 0.5, peak + jnp.log(whole), 0.0)
    evidence = pltpu.roll(jnp.broadcast_to(evidence, evid_ref.shape), lax.rem(128 - core * SLAB, 128), 1)
    evid_ref[...] = evidence

    def project(weights, block):
        data = lax.dot_general(
            weights[...], shifted[block], contract_plain, preferred_element_type=F32
        )
        weight = lax.dot_general(
            weights[:, 512:640], ctf[block], contract_plain, preferred_element_type=F32
        )
        return data, weight

    def place(r):
        return ring4(y, r // 4) * 4 + ring4(x, lax.rem(r, 4))

    def own_step(r, carry):
        data, weight = project(post, z_lo * 16 + place(r))
        acc[r, :, 0:256] = data
        acc[r, :, 256:384] = weight
        return carry

    def next_step(r):
        data, weight = project(post_z, 32 + place(r))
        acc[r, :, 0:256] += data
        acc[r, :, 256:384] += weight

    lax.fori_loop(0, 16, own_step, 0)
    arrived(POST, post_z)

    edge = COLS // 2

    def piece(half, slot, target, first, added=None):
        rows = slice(half * edge, half * edge + edge)

        def step(i, carry):
            other = first + i
            value = acc[other * 4 + target if half == 0 else target * 4 + other, rows, :]
            if added is not None:
                value = value + recv1[half, added, i].astype(F32)
            send1[half, slot, i] = value.astype(BF16)
            return carry

        lax.fori_loop(0, 2, step, 0)
        send(
            RS_1 + 6 * half + slot, send1.at[half, slot], recv1.at[half, slot],
            along(half, 1 if slot % 2 == 0 else -1),
        )

    def loop(count, index):
        def step(k, carry):
            next_step(index(k))
            return carry

        lax.fori_loop(0, count, step, 0)

    loop(4, lambda k: k * 4 + 2)
    piece(0, 0, 2, 0)
    piece(0, 1, 2, 2)
    loop(3, lambda k: 8 + k + k // 2)
    piece(1, 0, 2, 0)
    piece(1, 1, 2, 2)
    loop(9, lambda k: (k // 3 + k // 6) * 4 + lax.rem(k, 3) + lax.rem(k, 3) // 2)
    for half in (0, 1):
        piece(half, 2, 1, 2)
        piece(half, 3, 3, 0)
    for half in (0, 1):
        arrived(RS_1 + 6 * half, recv1.at[half, 0])
        piece(half, 4, 1, 0, 0)
        arrived(RS_1 + 6 * half + 1, recv1.at[half, 1])
        piece(half, 5, 3, 2, 1)

    def relay_rows(half, top):
        start = half * edge + top * ORIENTS
        return slice(start, start + ORIENTS)

    def relay(half, slot, distance, top, added=None):
        r = distance * 4 if half == 0 else distance
        value = acc[r, relay_rows(half, top), :]
        if added is not None:
            arrived(RS_2 + 6 * half + added, recv2.at[half, added])
            value = value + recv2[half, added]
        send2[half, slot] = value
        send(
            RS_2 + 6 * half + slot, send2.at[half, slot], recv2.at[half, slot],
            along(1 - half, 1 if slot % 2 == 0 else -1),
        )

    for half in (0, 1):
        rows = slice(half * edge, half * edge + edge)
        for slot in range(2, 6):
            arrived(RS_1 + 6 * half + slot, recv1.at[half, slot])
        for other in (2, 1, 3, 0):
            r = other * 4 if half == 0 else other
            i = other % 2
            near, far = (3, 4) if other < 2 else (2, 5)
            acc[r, rows, :] += recv1[half, near, i].astype(F32) + recv1[half, far, i].astype(F32)
        relay(half, 0, 2, 0)
        relay(half, 1, 2, 1)
        relay(half, 2, 1, 1)
        relay(half, 3, 3, 0)
    for half in (0, 1):
        relay(half, 4, 1, 0, 0)
        relay(half, 5, 3, 1, 1)

    for half in (0, 1):
        for slot in range(2, 6):
            arrived(RS_2 + 6 * half + slot, recv2.at[half, slot])
        sums2[half * 2] = acc[0, relay_rows(half, 0), :] + recv2[half, 3] + recv2[half, 4]
        sums2[half * 2 + 1] = acc[0, relay_rows(half, 1), :] + recv2[half, 2] + recv2[half, 5]

    middle = ORIENTS // 2

    def pass_on(slot, distance, top, added=None):
        value = sums2[ring4(z_hi, distance), top * middle:(top + 1) * middle, :]
        if added is not None:
            arrived(RS_Z + added, recv3.at[added])
            value = value + recv3[added]
        send3[slot] = value
        to = ring4(z_hi, 1 if slot % 2 == 0 else -1)
        send(RS_Z + slot, send3.at[slot], recv3.at[slot], device(y, x, to * 2 + z_lo))

    pass_on(0, 2, 0)
    pass_on(1, 2, 1)
    pass_on(2, 1, 1)
    pass_on(3, -1, 0)
    pass_on(4, 1, 0, 0)
    pass_on(5, -1, 1, 1)
    for slot in range(2, 6):
        arrived(RS_Z + slot, recv3.at[slot])
    for top in (0, 1):
        rows = slice(top * middle, (top + 1) * middle)
        near, far = ((3, 4), (2, 5))[top]
        total = sums2[z_hi, rows, :] + recv3[near] + recv3[far]
        divisor = total[:, 256:384] + WIENER_TERM
        est_ref[rows, 0:128] = total[:, 0:128] / divisor
        est_ref[rows, 128:256] = total[:, 128:256] / divisor

    for item in pending:
        item.wait_send()


def on_device(particles, defocus, orient, center, live, sigma2, projections):
    images = particles.reshape(SLAB, 2, 16, 2, 128).transpose(3, 1, 0, 2, 4).reshape(2, 2, SLAB, 2048)
    vmem = pl.BlockSpec(memory_space=pltpu.VMEM)
    estimate, evidence = pl.pallas_call(
        kernel,
        out_shape=(
            jax.ShapeDtypeStruct((ORIENTS, 256), F32),
            jax.ShapeDtypeStruct((8, 128), F32),
        ),
        in_specs=[vmem] * 7,
        out_specs=(vmem, vmem),
        scratch_shapes=[
            pltpu.VMEM((NY, NX, NL, NH, ORIENTS, 256), BF16),
            pltpu.VMEM((3, 2, 2, SLAB, 2048), BF16),
            pltpu.VMEM((2, 2, SLAB, 128), F32),
            pltpu.VMEM((2, 24, 128), F32),
            pltpu.VMEM((128, 128), F32),
            pltpu.VMEM((5, BLOCKS, 128), F32),
            pltpu.VMEM((2, 8, 128), F32),
            pltpu.VMEM((48, ROWS, 256), BF16),
            pltpu.VMEM((48, 128, 128), BF16),
            pltpu.VMEM((ROWS, 256), F32),
            pltpu.VMEM((COLS, 128), F32),
            pltpu.VMEM((COLS, ROWS), F32),
            pltpu.VMEM((COLS, ROWS), BF16),
            pltpu.VMEM((COLS, ROWS), BF16),
            pltpu.VMEM((16, COLS, 384), F32),
            pltpu.VMEM((2, 6, 2, COLS // 2, 384), BF16),
            pltpu.VMEM((2, 6, 2, COLS // 2, 384), BF16),
            pltpu.VMEM((2, 6, ORIENTS, 384), F32),
            pltpu.VMEM((2, 6, ORIENTS, 384), F32),
            pltpu.VMEM((NH, ORIENTS, 384), F32),
            pltpu.VMEM((6, ORIENTS // 2, 384), F32),
            pltpu.VMEM((6, ORIENTS // 2, 384), F32),
            pltpu.SemaphoreType.DMA((COPIES,)),
            pltpu.SemaphoreType.DMA((COPIES,)),
            pltpu.SemaphoreType.DMA((2,)),
        ],
        compiler_params=pltpu.CompilerParams(
            collective_id=0, has_side_effects=True, vmem_limit_bytes=50 * 1024 * 1024
        ),
    )(
        images, orient.T, center.reshape(1, SLAB), defocus.reshape(1, SLAB), live.reshape(1, 1),
        sigma2.reshape(BLOCKS, 128), projections.reshape(ORIENTS, 256),
    )
    return (estimate.reshape(1, ORIENTS, 2, 128), evidence[0, 0:SLAB])


def solution(mesh):
    return jax.shard_map(
        on_device,
        mesh=mesh,
        in_specs=(
            P(("dom", "cls"), None, None),
            P(("dom", "cls")),
            P(("dom", "cls"), None),
            P(("dom", "cls")),
            P(("dom", "cls")),
            P(),
            P("cls", None, None, "dom"),
        ),
        out_specs=(P("cls", None, None, "dom"), P(("dom", "cls"))),
        check_vma=False,
    )
```

```python
import math

import jax
import jax.numpy as jnp
from jax import lax
from jax.experimental import pallas as pl
from jax.experimental.pallas import tpu as pltpu
from jax.sharding import PartitionSpec as P

FSIDE = 64
BOX = 128
GRID = 9
SHIFTS = 9
ORIENTS = 48
CANDS = 16
SLAB = 32

CTF_GAIN = 400.0
CTF_PHASE = 0.07
WIENER_TERM = 0.002

NX, NY, NH = 4, 4, 4
BLOCKS = 32
COLS = NH * ORIENTS
PAIR = 2 * SLAB
ROWS = 640
MESH = pl.DeviceIdType.MESH
F32, BF16 = jnp.float32, jnp.bfloat16

SIN_TERMS = (6.2831853025115025, -41.34170040531776, 81.60513138580835, -76.70301535406267,
             42.02592698764344, -14.899846674846755, 3.2381375198594955)
COS_TERMS = (0.9999999890590235, -19.73920449945402, 64.93911745989969, -85.45013953094733,
             60.16763095140483, -25.96759924996967, 6.5286581631738425)

AG_Z = 0
AG_2 = 3
AG_3 = 11
PART, PART_Z, PART_F = 35, 36, 37
AUX, AUX_Z, AUX_F = 38, 39, 40
SCORE, NORM, POST = 41, 42, 43
RS_1 = 44
RS_2 = 60
RS_Z = 72
COPIES = 78


def poly(terms, x):
    total = terms[-1] * x + terms[-2]
    for term in terms[-3::-1]:
        total = total * x + term
    return total


def sin_turns(t):
    return poly(SIN_TERMS, t * t) * t


def cos_turns(t):
    return poly(COS_TERMS, t * t)


def kernel(
    part_ref, orient_ref, center_ref, defocus_ref, live_ref, sigma_ref, proj_ref,
    est_ref, evid_ref,
    gath, imgs, aux, wide, tables, norm, shifted, ctf, corr, power_sum, expo, next_scores,
    few, few_in, few_post, few_post_in, post, post_z,
    acc, send1, recv1, send2, recv2, sums2, send3, recv3,
    send_sem, recv_sem, local_sem,
):
    dom, cls = lax.axis_index("dom"), lax.axis_index("cls")
    z_lo, x, y = lax.rem(dom, 2), lax.rem(dom // 2, 4), dom // 8
    core, z_hi = lax.rem(cls, 2), cls // 2
    z = z_hi * 2 + z_lo

    def device(yy, xx, zz):
        return ((yy * NX + xx) * 2 + lax.rem(zz, 2), (zz // 2) * 2 + core)

    def ring4(position, step):
        return lax.rem(position + step + 4, 4)

    def along(axis, step):
        if axis == 0:
            return device(y, ring4(x, step), z)
        return device(ring4(y, step), x, z)

    here = (x, y)
    partner = (dom, z_hi * 2 + 1 - core)
    beside = device(y, x, z_hi * 2 + 1 - z_lo)

    def along_z(step):
        return device(y, x, ring4(z_hi, step) * 2 + z_lo)

    def copy(index, source, target, to):
        return pltpu.make_async_remote_copy(
            src_ref=source, dst_ref=target, send_sem=send_sem.at[index],
            recv_sem=recv_sem.at[index], device_id=to, device_id_type=MESH,
        )

    pending = []

    def send(index, source, target, to):
        out = copy(index, source, target, to)
        out.start()
        pending.append(out)

    def arrived(index, target):
        copy(index, target, target, partner).wait_recv()

    barrier = pltpu.get_barrier_semaphore()
    friends = [partner, beside]
    friends += [along(axis, step) for axis in (0, 1) for step in (1, -1)]
    friends += [along_z(step) for step in range(1, NH)]
    for friend in friends:
        pl.semaphore_signal(barrier, inc=1, device_id=friend, device_id_type=MESH)

    own = [
        pltpu.make_async_copy(part_ref.at[z_lo], imgs.at[0, core], local_sem.at[0]),
        pltpu.make_async_copy(proj_ref, gath.at[y, x, z_hi], local_sem.at[1]),
    ]
    for item in own:
        item.start()
    pl.semaphore_wait(barrier, len(friends))

    mine = gath.at[y, x, z_hi]
    for step in range(1, NH):
        send(AG_Z + step - 1, proj_ref, mine, along_z(step))
    send(PART, part_ref.at[z_lo], imgs.at[0, core], partner)

    center = center_ref[...].astype(F32)
    center_y = jnp.floor((center + 0.5) * (1.0 / (GRID - 2)))
    center_x = center - center_y * (GRID - 2)
    slot = lax.broadcasted_iota(jnp.int32, (1, SLAB), 1)
    wide[...] = jnp.zeros_like(wide)
    wide[0:CANDS, 0:SLAB] = orient_ref[...].astype(F32)
    wide[16:17, 0:SLAB] = jnp.where(slot < live_ref[...], 1.0, 0.0)
    wide[17:18, 0:SLAB] = CTF_GAIN * defocus_ref[...].astype(F32)
    wide[18:19, 0:SLAB] = center_x + (1 - GRID // 2)
    wide[19:20, 0:SLAB] = center_y + (1 - GRID // 2)
    placed = pltpu.roll(wide[0:24, :], core * SLAB, 1)
    aux[0, core, 0:24, :] = placed + pltpu.roll(placed, 64, 1)
    aux[0, core, 24:56, :] = jnp.transpose(wide[...])[0:SLAB, :]
    send(AUX, aux.at[0, core], aux.at[0, core], partner)
    send(AUX_Z, aux.at[0, core], aux.at[1, core], beside)

    block_row = lax.broadcasted_iota(jnp.int32, (BLOCKS, 128), 0)
    lane = lax.broadcasted_iota(jnp.int32, (BLOCKS, 128), 1)
    v_all = (block_row * 2 + lane // FSIDE - FSIDE // 2).astype(F32)
    u_all = lax.rem(lane, FSIDE).astype(F32)
    tables[0] = (u_all * u_all + v_all * v_all) * (1.0 / (BOX * BOX))
    tables[1] = v_all
    tables[2] = cos_turns(v_all * (1.0 / BOX))
    tables[3] = sin_turns(v_all * (1.0 / BOX))
    tables[4] = 1.0 / sigma_ref[...]
    u = u_all[0:1, :]
    cos_u, sin_u = cos_turns(u * (1.0 / BOX)), sin_turns(u * (1.0 / BOX))
    for item in own:
        item.wait()

    def shift_tile(group, owner, tile):
        start = tile * 16
        info = aux[group, owner, 24 + start:40 + start, :]
        gain, t_x, t_y = info[:, 17:18], info[:, 18:19], info[:, 19:20]
        base_turn = u * t_x
        row0 = owner * SLAB + start

        def rows_at(base):
            return pl.ds(pl.multiple_of(base + row0, 16), 16)

        def step(at_yx, carry):
            d = at_yx * 2 + z_lo
            block = group * 16 + at_yx
            radius = tables[0, pl.ds(d, 1), :]
            v = tables[1, pl.ds(d, 1), :]
            cos_v = tables[2, pl.ds(d, 1), :]
            sin_v = tables[3, pl.ds(d, 1), :]
            inverse = tables[4, pl.ds(d, 1), :]
            lanes = pl.ds(pl.multiple_of(at_yx * 128, 128), 128)
            real = imgs[group, owner, 0, pl.ds(start, 16), lanes].astype(F32)
            imag = imgs[group, owner, 1, pl.ds(start, 16), lanes].astype(F32)
            angle = gain * radius + CTF_PHASE
            turns = jnp.floor(angle * (0.5 / math.pi) + 0.5)
            rest = (angle - turns * 6.28125) - turns * 0.0019353071795864769
            contrast = -sin_turns(rest * (0.5 / math.pi))
            weight = contrast * inverse
            ctf_weight = (contrast * contrast * inverse).astype(BF16)
            ctf[block, rows_at(PAIR), :] = ctf_weight
            turn = (base_turn + v * t_y) * (1.0 / BOX)
            turn = turn - jnp.floor(turn + 0.5)
            cosine, sine = cos_turns(turn), sin_turns(turn)
            real, imag = real * weight, imag * weight
            mid = (real * cosine - imag * sine, real * sine + imag * cosine)

            def rotations(value, cos_, sin_):
                re, im = value
                re_c, re_s, im_c, im_s = re * cos_, re * sin_, im * cos_, im * sin_
                return ((re_c + im_s, im_c - re_s), value, (re_c - im_s, im_c + re_s))

            for d_y, moved in enumerate(rotations(mid, cos_v, sin_v)):
                for d_x, (re, im) in enumerate(rotations(moved, cos_u, sin_u)):
                    at = rows_at((d_y * 3 + d_x) * PAIR)
                    shifted[block, at, 0:128] = re.astype(BF16)
                    shifted[block, at, 128:256] = im.astype(BF16)
            return carry

        lax.fori_loop(0, 16, step, 0, unroll=4)

    def zero_step(block, carry):
        shifted[block, SHIFTS * PAIR:, :] = jnp.zeros((ROWS - SHIFTS * PAIR, 256), BF16)
        ctf[block, 0:PAIR, :] = jnp.zeros((PAIR, 128), BF16)
        return carry

    def view(half, position, part=None):
        cut = pl.ds(half * 2, 2) if part is None else pl.ds(half * 2 + part, 1)
        if half == 0:
            return gath.at[y, position, cut]
        return gath.at[position, x, cut]

    def view_piece(half, piece, position):
        cut = pl.ds(half * 2, 2)
        if half == 0:
            return gath.at[position, ring4(x, piece), cut]
        return gath.at[ring4(y, piece), position, cut]

    def ring_first(half):
        ref = view(half, here[half])
        send(AG_2 + 4 * half, ref, ref, along(half, 1))
        send(AG_2 + 4 * half + 1, ref, ref, along(half, -1))

    def ring_second(half):
        base = AG_2 + 4 * half
        left, right = ring4(here[half], -1), ring4(here[half], 1)
        arrived(base, view(half, left))
        ref = view(half, left, 0)
        send(base + 2, ref, ref, along(half, 1))
        arrived(base + 1, view(half, right))
        ref = view(half, right, 1)
        send(base + 3, ref, ref, along(half, -1))

    def ring_end(half):
        far = ring4(here[half], 2)
        arrived(AG_2 + 4 * half + 2, view(half, far, 0))
        arrived(AG_2 + 4 * half + 3, view(half, far, 1))

    def piece_first(half, piece):
        axis = 1 - half
        base = AG_3 + 12 * half + 3 * piece
        ref = view_piece(half, piece, here[axis])
        send(base, ref, ref, along(axis, 1))
        send(base + 1, ref, ref, along(axis, -1))

    def piece_second(half, piece):
        axis = 1 - half
        base = AG_3 + 12 * half + 3 * piece
        left = view_piece(half, piece, ring4(here[axis], -1))
        right = view_piece(half, piece, ring4(here[axis], 1))
        if piece % 2 == 0:
            arrived(base, left)
            send(base + 2, left, left, along(axis, 1))
            arrived(base + 1, right)
        else:
            arrived(base + 1, right)
            send(base + 2, right, right, along(axis, -1))
            arrived(base, left)

    def piece_end(half, piece):
        axis = 1 - half
        far = view_piece(half, piece, ring4(here[axis], 2))
        arrived(AG_3 + 12 * half + 3 * piece + 2, far)

    contract_last = (((1,), (1,)), ((), ()))
    contract_plain = (((1,), (0,)), ((), ()))

    def score(blocks, kinds=(0, 1)):
        volumes = [gath[yy, xx].reshape(COLS, 256) for yy, xx in blocks]
        squares = []
        for volume in volumes:
            re, im = volume[:, 0:128].astype(F32), volume[:, 128:256].astype(F32)
            squares.append((re * re + im * im).astype(BF16))
        for kind in kinds:
            total = power = None
            for (yy, xx), volume, squared in zip(blocks, volumes, squares):
                block = kind * 16 + yy * 4 + xx
                term = lax.dot_general(
                    shifted[block], volume, contract_last, preferred_element_type=F32
                )
                term_p = lax.dot_general(
                    squared, ctf[block], contract_last, preferred_element_type=F32
                )
                total = term if total is None else total + term
                power = term_p if power is None else power + term_p
            corr[kind, :, 0:COLS] += total
            power_sum[kind] += power

    def near_step(k, carry):
        yy = ring4(y, k + k // 2)
        score([(yy, ring4(x, dx)) for dx in (0, 1, 3)])
        return carry

    def far_step(k, carry):
        step = k + k // 2
        score([(ring4(y, step), ring4(x, 2)), (ring4(y, 2), ring4(x, step))])
        return carry

    shift_tile(0, core, 0)
    shift_tile(0, core, 1)
    for step in range(1, NH):
        arrived(AG_Z + step - 1, gath.at[y, x, ring4(z_hi, -step)])
    for half in (0, 1):
        ring_first(half)
    for half in (0, 1):
        piece_first(half, 0)
    send(PART_Z, part_ref.at[1 - z_lo], imgs.at[1, core], beside)
    arrived(PART, imgs.at[0, 1 - core])
    arrived(AUX, aux.at[0, 1 - core])
    shift_tile(0, 1 - core, 0)
    for half in (0, 1):
        ring_second(half)
    for half in (0, 1):
        piece_first(half, 1)
        piece_first(half, 3)
    shift_tile(0, 1 - core, 1)
    for half in (0, 1):
        ring_end(half)
        piece_first(half, 2)
    for half in (0, 1):
        piece_second(half, 0)
    lax.fori_loop(0, 32, zero_step, 0)
    corr[...] = jnp.zeros_like(corr)
    power_sum[...] = jnp.zeros_like(power_sum)
    arrived(PART_Z, imgs.at[1, core])
    send(PART_F, imgs.at[1, core], imgs.at[1, core], partner)
    arrived(AUX_Z, aux.at[1, core])
    send(AUX_F, aux.at[1, core], aux.at[1, core], partner)
    shift_tile(1, core, 0)
    for half in (0, 1):
        piece_second(half, 1)
        piece_second(half, 3)
    shift_tile(1, core, 1)
    arrived(PART_F, imgs.at[1, 1 - core])
    arrived(AUX_F, aux.at[1, 1 - core])
    shift_tile(1, 1 - core, 0)
    for half in (0, 1):
        piece_second(half, 2)
    shift_tile(1, 1 - core, 1)
    lax.fori_loop(0, 3, near_step, 0)
    for half in (0, 1):
        for piece in (0, 1, 3):
            piece_end(half, piece)
    lax.fori_loop(0, 3, far_step, 0)
    for half in (0, 1):
        piece_end(half, 2)
    last = [(ring4(y, 2), ring4(x, 2))]
    score(last, (1,))

    def turn(kind, target):
        power_term = 0.5 * (power_sum[kind] + pltpu.roll(power_sum[kind], 64, 1))
        for tile in range(5):
            lanes = slice(tile * 128, tile * 128 + 128)
            target[:, lanes] = jnp.transpose(corr[kind, lanes, :])[0:COLS, :] - power_term

    row = lax.broadcasted_iota(jnp.int32, (ORIENTS, 128), 0).astype(F32)
    wide[32:56, :] = aux[1, 0, 0:24, :] + aux[1, 1, 0:24, :]
    turn(1, next_scores)

    def candidates(source, base):
        def few_step(j, carry):
            chosen = wide[pl.ds(base + j, 1), :] == row
            for h in range(NH):
                for tile in range(5):
                    part = source[h * ORIENTS:(h + 1) * ORIENTS, tile * 128:tile * 128 + 128]
                    value = jnp.sum(jnp.where(chosen, part, 0.0), axis=0, keepdims=True)
                    few[h * 5 + tile, pl.ds(j, 1), :] = value
            return carry

        lax.fori_loop(0, CANDS, few_step, 0)

    candidates(next_scores, 32)
    score_sent = copy(SCORE, few, few_in, beside)
    score_sent.start()
    score(last, (0,))
    turn(0, expo)

    info = aux[0, 0, 0:24, :] + aux[0, 1, 0:24, :]
    wide[64:88, :] = info
    allowed = jnp.zeros((ORIENTS, 128), jnp.bool_)
    for j in range(CANDS):
        allowed = allowed | (info[j:j + 1, :] == row)
    allowed = jnp.where(allowed, 1.0, 0.0)
    allowed = jnp.concatenate([allowed] * NH, axis=0) > 0.5
    lower = lax.broadcasted_iota(jnp.int32, (COLS, 128), 1) < PAIR
    live = info[CANDS:CANDS + 1, :]
    least = jnp.float32(-3.0e38)
    arrived(SCORE, few_in)

    def spread(h, source, base):
        added = [jnp.zeros((ORIENTS, 128), F32) for _ in range(5)]
        for j in range(CANDS):
            chosen = wide[base + j:base + j + 1, :] == row
            for tile in range(5):
                value = source[h * 5 + tile, j:j + 1, :]
                added[tile] = jnp.where(chosen, value, added[tile])
        return added

    def class_rows(h):
        return pl.ds(pl.multiple_of(h * ORIENTS, 16), ORIENTS)

    def spread_step(h, carry):
        for tile, added in enumerate(spread(h, few_in, 64)):
            expo[class_rows(h), tile * 128:tile * 128 + 128] += added
        return carry

    lax.fori_loop(0, NH, spread_step, 0)
    highest = jnp.full((1, 128), least, F32)
    for tile in range(5):
        lanes = slice(tile * 128, tile * 128 + 128)
        valid = allowed & lower if tile == 4 else allowed
        scores = jnp.where(valid, expo[:, lanes], least)
        highest = jnp.maximum(highest, jnp.max(scores, axis=0, keepdims=True))
    highest = jnp.maximum(highest, pltpu.roll(highest, 64, 1))
    partition = jnp.zeros((1, 128), F32)
    for tile in range(5):
        lanes = slice(tile * 128, tile * 128 + 128)
        valid = allowed & lower if tile == 4 else allowed
        terms = jnp.where(valid, jnp.exp(expo[:, lanes] - highest), 0.0)
        expo[:, lanes] = terms
        partition = partition + jnp.sum(terms, axis=0, keepdims=True)
    partition = partition + pltpu.roll(partition, 64, 1)

    norm[core, 0:1, :] = highest
    norm[core, 1:2, :] = partition
    norm[core, 2:8, :] = jnp.zeros((6, 128), F32)
    send(NORM, norm.at[core], norm.at[core], partner)
    arrived(NORM, norm.at[1 - core])
    other = norm[1 - core]
    peak = jnp.maximum(highest, other[0:1, :])
    mine_scale = jnp.exp(highest - peak)
    whole = partition * mine_scale + other[1:2, :] * jnp.exp(other[0:1, :] - peak)
    scale = jnp.where(live > 0.5, mine_scale / whole, 0.0)
    mass = jnp.zeros((COLS, 128), F32)
    for tile in range(5):
        lanes = slice(tile * 128, tile * 128 + 128)
        posterior = (expo[:, lanes] * scale).astype(BF16).astype(F32)
        mass = mass + posterior
        expo[:, lanes] = posterior
        if tile == 4:
            mass = mass + pltpu.roll(mass, 64, 1)
            posterior = jnp.where(lower, posterior, mass)
        post[:, lanes] = posterior.astype(BF16)
    score_sent.wait_send()
    candidates(expo, 64)
    few_post[...] = few[...].astype(BF16)
    send(POST, few_post, few_post_in, beside)
    evidence = jnp.where(live > 0.5, peak + jnp.log(whole), 0.0)
    evidence = pltpu.roll(jnp.broadcast_to(evidence, evid_ref.shape), lax.rem(128 - core * SLAB, 128), 1)
    evid_ref[...] = evidence

    def project(weights, block):
        data = lax.dot_general(
            weights[...], shifted[block], contract_plain, preferred_element_type=F32
        )
        weight = lax.dot_general(
            weights[:, 512:640], ctf[block], contract_plain, preferred_element_type=F32
        )
        return data, weight

    def place(r):
        return ring4(y, r // 4) * 4 + ring4(x, lax.rem(r, 4))

    def own_step(r, carry):
        data, weight = project(post, place(r))
        acc[r, :, 0:256] = data
        acc[r, :, 256:384] = weight
        return carry

    def next_step(r):
        data, weight = project(post_z, 16 + place(r))
        acc[r, :, 0:256] += data
        acc[r, :, 256:384] += weight

    lax.fori_loop(0, 16, own_step, 0)
    arrived(POST, few_post_in)
    few_in[...] = few_post_in[...].astype(F32)
    lower_part = lax.broadcasted_iota(jnp.int32, (ORIENTS, 128), 1) < PAIR

    def spread_post(h, carry):
        mass = jnp.zeros((ORIENTS, 128), F32)
        for tile, value in enumerate(spread(h, few_in, 32)):
            mass = mass + value
            if tile == 4:
                mass = mass + pltpu.roll(mass, 64, 1)
                value = jnp.where(lower_part, value, mass)
            post_z[class_rows(h), tile * 128:tile * 128 + 128] = value.astype(BF16)
        return carry

    lax.fori_loop(0, NH, spread_post, 0)

    edge = COLS // 2

    def pack(half, slot, i, target, other, added=None):
        rows = slice(half * edge, half * edge + edge)
        value = acc[other * 4 + target if half == 0 else target * 4 + other, rows, :]
        if added is not None:
            value = value + recv1[half, added, i].astype(F32)
        send1[half, slot, i] = value.astype(BF16)

    def piece(half, slot, target, first):
        for i in (0, 1):
            pack(half, slot, i, target, first + i)
        send(
            RS_1 + 8 * half + slot, send1.at[half, slot], recv1.at[half, slot],
            along(half, 1 if slot % 2 == 0 else -1),
        )

    def piece_sum(half, slot, i, target, other, added):
        pack(half, slot, i, target, other, added)
        send(
            RS_1 + 8 * half + 2 * slot - 4 + i, send1.at[half, slot, i], recv1.at[half, slot, i],
            along(half, 1 if slot % 2 == 0 else -1),
        )

    def loop(count, index):
        def step(k, carry):
            next_step(index(k))
            return carry

        lax.fori_loop(0, count, step, 0)

    loop(4, lambda k: k * 4 + 2)
    piece(0, 0, 2, 0)
    piece(0, 1, 2, 2)
    loop(3, lambda k: 8 + k + k // 2)
    piece(1, 0, 2, 0)
    piece(1, 1, 2, 2)
    loop(9, lambda k: (k // 3 + k // 6) * 4 + lax.rem(k, 3) + lax.rem(k, 3) // 2)
    for half in (0, 1):
        piece(half, 2, 1, 2)
        piece(half, 3, 3, 0)
    for half in (0, 1):
        arrived(RS_1 + 8 * half + 1, recv1.at[half, 1])
        piece_sum(half, 5, 0, 3, 2, 1)
        arrived(RS_1 + 8 * half, recv1.at[half, 0])
        piece_sum(half, 4, 1, 1, 1, 0)
    for half in (0, 1):
        piece_sum(half, 5, 1, 3, 3, 1)
        piece_sum(half, 4, 0, 1, 0, 0)

    def relay_rows(half, top):
        start = half * edge + top * ORIENTS
        return slice(start, start + ORIENTS)

    def relay(half, slot, distance, top, added=None):
        r = distance * 4 if half == 0 else distance
        value = acc[r, relay_rows(half, top), :]
        if added is not None:
            arrived(RS_2 + 6 * half + added, recv2.at[half, added])
            value = value + recv2[half, added]
        send2[half, slot] = value
        send(
            RS_2 + 6 * half + slot, send2.at[half, slot], recv2.at[half, slot],
            along(1 - half, 1 if slot % 2 == 0 else -1),
        )

    for other in (2, 1, 3, 0):
        i = other % 2
        whole_slot, split_slot = (3, 4) if other < 2 else (2, 5)
        for half in (0, 1):
            rows = slice(half * edge, half * edge + edge)
            if other in (1, 2):
                arrived(RS_1 + 8 * half + whole_slot, recv1.at[half, whole_slot])
            arrived(RS_1 + 8 * half + 2 * split_slot - 4 + i, recv1.at[half, split_slot, i])
            r = other * 4 if half == 0 else other
            acc[r, rows, :] += (
                recv1[half, whole_slot, i].astype(F32) + recv1[half, split_slot, i].astype(F32)
            )
            if other == 2:
                relay(half, 0, 2, 0)
                relay(half, 1, 2, 1)
            elif other == 1:
                relay(half, 2, 1, 1)
            elif other == 3:
                relay(half, 3, 3, 0)
    for half in (0, 1):
        relay(half, 4, 1, 0, 0)
        relay(half, 5, 3, 1, 1)

    for half in (0, 1):
        for slot in range(2, 6):
            arrived(RS_2 + 6 * half + slot, recv2.at[half, slot])
        sums2[half * 2] = acc[0, relay_rows(half, 0), :] + recv2[half, 3] + recv2[half, 4]
        sums2[half * 2 + 1] = acc[0, relay_rows(half, 1), :] + recv2[half, 2] + recv2[half, 5]

    middle = ORIENTS // 2

    def pass_on(slot, distance, top, added=None):
        value = sums2[ring4(z_hi, distance), top * middle:(top + 1) * middle, :]
        if added is not None:
            arrived(RS_Z + added, recv3.at[added])
            value = value + recv3[added]
        send3[slot] = value
        to = along_z(1 if slot % 2 == 0 else -1)
        send(RS_Z + slot, send3.at[slot], recv3.at[slot], to)

    pass_on(0, 2, 0)
    pass_on(1, 2, 1)
    pass_on(2, 1, 1)
    pass_on(3, -1, 0)
    pass_on(4, 1, 0, 0)
    pass_on(5, -1, 1, 1)
    for slot in range(2, 6):
        arrived(RS_Z + slot, recv3.at[slot])
    for top in (0, 1):
        rows = slice(top * middle, (top + 1) * middle)
        near, far = ((3, 4), (2, 5))[top]
        total = sums2[z_hi, rows, :] + recv3[near] + recv3[far]
        divisor = total[:, 256:384] + WIENER_TERM
        est_ref[rows, 0:128] = total[:, 0:128] / divisor
        est_ref[rows, 128:256] = total[:, 128:256] / divisor

    for item in pending:
        item.wait_send()


def on_device(particles, defocus, orient, center, live, sigma2, projections):
    images = particles.reshape(SLAB, 2, 16, 2, 128).transpose(3, 1, 0, 2, 4).reshape(2, 2, SLAB, 2048)
    vmem = pl.BlockSpec(memory_space=pltpu.VMEM)
    estimate, evidence = pl.pallas_call(
        kernel,
        out_shape=(
            jax.ShapeDtypeStruct((ORIENTS, 256), F32),
            jax.ShapeDtypeStruct((8, 128), F32),
        ),
        in_specs=[vmem] * 7,
        out_specs=(vmem, vmem),
        scratch_shapes=[
            pltpu.VMEM((NY, NX, NH, ORIENTS, 256), BF16),
            pltpu.VMEM((2, 2, 2, SLAB, 2048), BF16),
            pltpu.VMEM((2, 2, 56, 128), F32),
            pltpu.VMEM((128, 128), F32),
            pltpu.VMEM((5, BLOCKS, 128), F32),
            pltpu.VMEM((2, 8, 128), F32),
            pltpu.VMEM((32, ROWS, 256), BF16),
            pltpu.VMEM((32, 128, 128), BF16),
            pltpu.VMEM((2, ROWS, 256), F32),
            pltpu.VMEM((2, COLS, 128), F32),
            pltpu.VMEM((COLS, ROWS), F32),
            pltpu.VMEM((COLS, ROWS), F32),
            pltpu.VMEM((5 * NH, CANDS, 128), F32),
            pltpu.VMEM((5 * NH, CANDS, 128), F32),
            pltpu.VMEM((5 * NH, CANDS, 128), BF16),
            pltpu.VMEM((5 * NH, CANDS, 128), BF16),
            pltpu.VMEM((COLS, ROWS), BF16),
            pltpu.VMEM((COLS, ROWS), BF16),
            pltpu.VMEM((16, COLS, 384), F32),
            pltpu.VMEM((2, 6, 2, COLS // 2, 384), BF16),
            pltpu.VMEM((2, 6, 2, COLS // 2, 384), BF16),
            pltpu.VMEM((2, 6, ORIENTS, 384), F32),
            pltpu.VMEM((2, 6, ORIENTS, 384), F32),
            pltpu.VMEM((NH, ORIENTS, 384), F32),
            pltpu.VMEM((6, ORIENTS // 2, 384), F32),
            pltpu.VMEM((6, ORIENTS // 2, 384), F32),
            pltpu.SemaphoreType.DMA((COPIES,)),
            pltpu.SemaphoreType.DMA((COPIES,)),
            pltpu.SemaphoreType.DMA((2,)),
        ],
        compiler_params=pltpu.CompilerParams(
            collective_id=0, has_side_effects=True, vmem_limit_bytes=50 * 1024 * 1024
        ),
    )(
        images, orient.T, center.reshape(1, SLAB), defocus.reshape(1, SLAB), live.reshape(1, 1),
        sigma2.reshape(BLOCKS, 128), projections.reshape(ORIENTS, 256),
    )
    return (estimate.reshape(1, ORIENTS, 2, 128), evidence[0, 0:SLAB])


def solution(mesh):
    return jax.shard_map(
        on_device,
        mesh=mesh,
        in_specs=(
            P(("dom", "cls"), None, None),
            P(("dom", "cls")),
            P(("dom", "cls"), None),
            P(("dom", "cls")),
            P(("dom", "cls")),
            P(),
            P("cls", None, None, "dom"),
        ),
        out_specs=(P("cls", None, None, "dom"), P(("dom", "cls"))),
        check_vma=False,
    )
```

```python
import math

import jax
import jax.numpy as jnp
from jax import lax
from jax.experimental import pallas as pl
from jax.experimental.pallas import tpu as pltpu
from jax.sharding import PartitionSpec as P

FSIDE = 64
BOX = 128
GRID = 9
SHIFTS = 9
ORIENTS = 48
CANDS = 16
SLAB = 32

CTF_GAIN = 400.0
CTF_PHASE = 0.07
WIENER_TERM = 0.002

NX, NY, NH = 4, 4, 4
BLOCKS = 32
COLS = NH * ORIENTS
PAIR = 2 * SLAB
ROWS = 640
MESH = pl.DeviceIdType.MESH
F32, BF16 = jnp.float32, jnp.bfloat16

SIN_TERMS = (6.2831853025115025, -41.34170040531776, 81.60513138580835, -76.70301535406267,
             42.02592698764344, -14.899846674846755, 3.2381375198594955)
COS_TERMS = (0.9999999890590235, -19.73920449945402, 64.93911745989969, -85.45013953094733,
             60.16763095140483, -25.96759924996967, 6.5286581631738425)

AG_Z = 0
AG_2 = 3
AG_3 = 11
PART, PART_Z, PART_F = 35, 36, 37
AUX, AUX_Z, AUX_F = 38, 39, 40
SCORE, NORM, POST = 41, 42, 43
RS_1 = 44
RS_2 = 60
RS_Z = 72
SCORE_2 = 78
COPIES = 79


def poly(terms, x):
    total = terms[-1] * x + terms[-2]
    for term in terms[-3::-1]:
        total = total * x + term
    return total


def sin_turns(t):
    return poly(SIN_TERMS, t * t) * t


def cos_turns(t):
    return poly(COS_TERMS, t * t)


def kernel(
    part_ref, orient_ref, center_ref, defocus_ref, live_ref, sigma_ref, proj_ref,
    est_ref, evid_ref,
    gath, imgs, aux, wide, tables, norm, shifted, ctf, corr, power_sum, expo, next_scores,
    few, few_in, few_post, few_post_in, post, post_z,
    acc, send1, recv1, send2, recv2, sums2, send3, recv3,
    send_sem, recv_sem, local_sem,
):
    dom, cls = lax.axis_index("dom"), lax.axis_index("cls")
    z_lo, x, y = lax.rem(dom, 2), lax.rem(dom // 2, 4), dom // 8
    core, z_hi = lax.rem(cls, 2), cls // 2
    z = z_hi * 2 + z_lo

    def device(yy, xx, zz):
        return ((yy * NX + xx) * 2 + lax.rem(zz, 2), (zz // 2) * 2 + core)

    def ring4(position, step):
        return lax.rem(position + step + 4, 4)

    def along(axis, step):
        if axis == 0:
            return device(y, ring4(x, step), z)
        return device(ring4(y, step), x, z)

    here = (x, y)
    partner = (dom, z_hi * 2 + 1 - core)
    beside = device(y, x, z_hi * 2 + 1 - z_lo)

    def along_z(step):
        return device(y, x, ring4(z_hi, step) * 2 + z_lo)

    def copy(index, source, target, to):
        return pltpu.make_async_remote_copy(
            src_ref=source, dst_ref=target, send_sem=send_sem.at[index],
            recv_sem=recv_sem.at[index], device_id=to, device_id_type=MESH,
        )

    pending = []

    def send(index, source, target, to):
        out = copy(index, source, target, to)
        out.start()
        pending.append(out)

    def arrived(index, target):
        copy(index, target, target, partner).wait_recv()

    barrier = pltpu.get_barrier_semaphore()
    friends = [partner, beside]
    friends += [along(axis, step) for axis in (0, 1) for step in (1, -1)]
    friends += [along_z(step) for step in range(1, NH)]
    for friend in friends:
        pl.semaphore_signal(barrier, inc=1, device_id=friend, device_id_type=MESH)

    own = [
        pltpu.make_async_copy(part_ref.at[z_lo], imgs.at[0, core], local_sem.at[0]),
        pltpu.make_async_copy(proj_ref, gath.at[y, x, z_hi], local_sem.at[1]),
    ]
    for item in own:
        item.start()
    pl.semaphore_wait(barrier, len(friends))

    mine = gath.at[y, x, z_hi]
    for step in range(1, NH):
        send(AG_Z + step - 1, proj_ref, mine, along_z(step))
    send(PART, part_ref.at[z_lo], imgs.at[0, core], partner)

    center = center_ref[...].astype(F32)
    center_y = jnp.floor((center + 0.5) * (1.0 / (GRID - 2)))
    center_x = center - center_y * (GRID - 2)
    slot = lax.broadcasted_iota(jnp.int32, (1, SLAB), 1)
    wide[...] = jnp.zeros_like(wide)
    wide[0:CANDS, 0:SLAB] = orient_ref[...].astype(F32)
    wide[16:17, 0:SLAB] = jnp.where(slot < live_ref[...], 1.0, 0.0)
    wide[17:18, 0:SLAB] = CTF_GAIN * defocus_ref[...].astype(F32)
    wide[18:19, 0:SLAB] = center_x + (1 - GRID // 2)
    wide[19:20, 0:SLAB] = center_y + (1 - GRID // 2)
    placed = pltpu.roll(wide[0:24, :], core * SLAB, 1)
    aux[0, core, 0:24, :] = placed + pltpu.roll(placed, 64, 1)
    aux[0, core, 24:56, :] = jnp.transpose(wide[...])[0:SLAB, :]
    send(AUX, aux.at[0, core], aux.at[0, core], partner)
    send(AUX_Z, aux.at[0, core], aux.at[1, core], beside)

    block_row = lax.broadcasted_iota(jnp.int32, (BLOCKS, 128), 0)
    lane = lax.broadcasted_iota(jnp.int32, (BLOCKS, 128), 1)
    v_all = (block_row * 2 + lane // FSIDE - FSIDE // 2).astype(F32)
    u_all = lax.rem(lane, FSIDE).astype(F32)
    tables[0] = (u_all * u_all + v_all * v_all) * (1.0 / (BOX * BOX))
    tables[1] = v_all
    tables[2] = cos_turns(v_all * (1.0 / BOX))
    tables[3] = sin_turns(v_all * (1.0 / BOX))
    tables[4] = 1.0 / sigma_ref[...]
    u = u_all[0:1, :]
    cos_u, sin_u = cos_turns(u * (1.0 / BOX)), sin_turns(u * (1.0 / BOX))
    for item in own:
        item.wait()

    def shift_tile(group, owner, tile):
        start = tile * 16
        info = aux[group, owner, 24 + start:40 + start, :]
        gain, t_x, t_y = info[:, 17:18], info[:, 18:19], info[:, 19:20]
        base_turn = u * t_x
        row0 = owner * SLAB + start

        def rows_at(base):
            return pl.ds(pl.multiple_of(base + row0, 16), 16)

        def step(at_yx, carry):
            d = at_yx * 2 + z_lo
            block = group * 16 + at_yx
            radius = tables[0, pl.ds(d, 1), :]
            v = tables[1, pl.ds(d, 1), :]
            cos_v = tables[2, pl.ds(d, 1), :]
            sin_v = tables[3, pl.ds(d, 1), :]
            inverse = tables[4, pl.ds(d, 1), :]
            lanes = pl.ds(pl.multiple_of(at_yx * 128, 128), 128)
            real = imgs[group, owner, 0, pl.ds(start, 16), lanes].astype(F32)
            imag = imgs[group, owner, 1, pl.ds(start, 16), lanes].astype(F32)
            angle = gain * radius + CTF_PHASE
            turns = jnp.floor(angle * (0.5 / math.pi) + 0.5)
            rest = (angle - turns * 6.28125) - turns * 0.0019353071795864769
            contrast = -sin_turns(rest * (0.5 / math.pi))
            weight = contrast * inverse
            ctf_weight = (contrast * contrast * inverse).astype(BF16)
            ctf[block, rows_at(PAIR), :] = ctf_weight
            turn = (base_turn + v * t_y) * (1.0 / BOX)
            turn = turn - jnp.floor(turn + 0.5)
            cosine, sine = cos_turns(turn), sin_turns(turn)
            real, imag = real * weight, imag * weight
            mid = (real * cosine - imag * sine, real * sine + imag * cosine)

            def rotations(value, cos_, sin_):
                re, im = value
                re_c, re_s, im_c, im_s = re * cos_, re * sin_, im * cos_, im * sin_
                return ((re_c + im_s, im_c - re_s), value, (re_c - im_s, im_c + re_s))

            for d_y, moved in enumerate(rotations(mid, cos_v, sin_v)):
                for d_x, (re, im) in enumerate(rotations(moved, cos_u, sin_u)):
                    at = rows_at((d_y * 3 + d_x) * PAIR)
                    shifted[block, at, 0:128] = re.astype(BF16)
                    shifted[block, at, 128:256] = im.astype(BF16)
            return carry

        lax.fori_loop(0, 16, step, 0, unroll=4)

    def zero_step(block, carry):
        shifted[block, SHIFTS * PAIR:, :] = jnp.zeros((ROWS - SHIFTS * PAIR, 256), BF16)
        ctf[block, 0:PAIR, :] = jnp.zeros((PAIR, 128), BF16)
        return carry

    def view(half, position, part=None):
        cut = pl.ds(half * 2, 2) if part is None else pl.ds(half * 2 + part, 1)
        if half == 0:
            return gath.at[y, position, cut]
        return gath.at[position, x, cut]

    def view_piece(half, piece, position):
        cut = pl.ds(half * 2, 2)
        if half == 0:
            return gath.at[position, ring4(x, piece), cut]
        return gath.at[ring4(y, piece), position, cut]

    def ring_first(half):
        ref = view(half, here[half])
        send(AG_2 + 4 * half, ref, ref, along(half, 1))
        send(AG_2 + 4 * half + 1, ref, ref, along(half, -1))

    def ring_second(half):
        base = AG_2 + 4 * half
        left, right = ring4(here[half], -1), ring4(here[half], 1)
        arrived(base, view(half, left))
        ref = view(half, left, 0)
        send(base + 2, ref, ref, along(half, 1))
        arrived(base + 1, view(half, right))
        ref = view(half, right, 1)
        send(base + 3, ref, ref, along(half, -1))

    def ring_end(half):
        far = ring4(here[half], 2)
        arrived(AG_2 + 4 * half + 2, view(half, far, 0))
        arrived(AG_2 + 4 * half + 3, view(half, far, 1))

    def piece_first(half, piece):
        axis = 1 - half
        base = AG_3 + 12 * half + 3 * piece
        ref = view_piece(half, piece, here[axis])
        send(base, ref, ref, along(axis, 1))
        send(base + 1, ref, ref, along(axis, -1))

    def piece_second(half, piece):
        axis = 1 - half
        base = AG_3 + 12 * half + 3 * piece
        left = view_piece(half, piece, ring4(here[axis], -1))
        right = view_piece(half, piece, ring4(here[axis], 1))
        if piece % 2 == 0:
            arrived(base, left)
            send(base + 2, left, left, along(axis, 1))
            arrived(base + 1, right)
        else:
            arrived(base + 1, right)
            send(base + 2, right, right, along(axis, -1))
            arrived(base, left)

    def piece_end(half, piece):
        axis = 1 - half
        far = view_piece(half, piece, ring4(here[axis], 2))
        arrived(AG_3 + 12 * half + 3 * piece + 2, far)

    contract_last = (((1,), (1,)), ((), ()))
    contract_plain = (((1,), (0,)), ((), ()))

    def score(blocks, kinds=(0, 1)):
        volumes = [gath[yy, xx].reshape(COLS, 256) for yy, xx in blocks]
        squares = []
        for volume in volumes:
            re, im = volume[:, 0:128].astype(F32), volume[:, 128:256].astype(F32)
            squares.append((re * re + im * im).astype(BF16))
        for kind in kinds:
            total = power = None
            for (yy, xx), volume, squared in zip(blocks, volumes, squares):
                block = kind * 16 + yy * 4 + xx
                term = lax.dot_general(
                    shifted[block], volume, contract_last, preferred_element_type=F32
                )
                term_p = lax.dot_general(
                    squared, ctf[block], contract_last, preferred_element_type=F32
                )
                total = term if total is None else total + term
                power = term_p if power is None else power + term_p
            corr[kind, :, 0:COLS] += total
            power_sum[kind] += power

    def near_step(k, carry):
        yy = ring4(y, k + k // 2)
        score([(yy, ring4(x, dx)) for dx in (0, 1, 3)])
        return carry

    def far_step(k, carry):
        step = k + k // 2
        score([(ring4(y, step), ring4(x, 2)), (ring4(y, 2), ring4(x, step))])
        return carry

    shift_tile(0, core, 0)
    shift_tile(0, core, 1)
    for step in range(1, NH):
        arrived(AG_Z + step - 1, gath.at[y, x, ring4(z_hi, -step)])
    for half in (0, 1):
        ring_first(half)
    for half in (0, 1):
        piece_first(half, 0)
    send(PART_Z, part_ref.at[1 - z_lo], imgs.at[1, core], beside)
    arrived(PART, imgs.at[0, 1 - core])
    arrived(AUX, aux.at[0, 1 - core])
    shift_tile(0, 1 - core, 0)
    for half in (0, 1):
        ring_second(half)
    for half in (0, 1):
        piece_first(half, 1)
        piece_first(half, 3)
    shift_tile(0, 1 - core, 1)
    for half in (0, 1):
        ring_end(half)
        piece_first(half, 2)
    for half in (0, 1):
        piece_second(half, 0)
    lax.fori_loop(0, 32, zero_step, 0)
    corr[...] = jnp.zeros_like(corr)
    power_sum[...] = jnp.zeros_like(power_sum)
    for half in (0, 1):
        piece_second(half, 1)
        piece_second(half, 3)
    arrived(PART_Z, imgs.at[1, core])
    send(PART_F, imgs.at[1, core], imgs.at[1, core], partner)
    arrived(AUX_Z, aux.at[1, core])
    send(AUX_F, aux.at[1, core], aux.at[1, core], partner)
    shift_tile(1, core, 0)
    for half in (0, 1):
        piece_second(half, 2)
    shift_tile(1, core, 1)
    arrived(PART_F, imgs.at[1, 1 - core])
    arrived(AUX_F, aux.at[1, 1 - core])
    shift_tile(1, 1 - core, 0)
    shift_tile(1, 1 - core, 1)
    lax.fori_loop(0, 3, near_step, 0)
    for half in (0, 1):
        for piece in (0, 1, 3):
            piece_end(half, piece)
    lax.fori_loop(0, 3, far_step, 0)
    for half in (0, 1):
        piece_end(half, 2)
    last = [(ring4(y, 2), ring4(x, 2))]
    score(last, (1,))

    def turn(kind, target):
        power_term = 0.5 * (power_sum[kind] + pltpu.roll(power_sum[kind], 64, 1))
        for tile in range(5):
            lanes = slice(tile * 128, tile * 128 + 128)
            target[:, lanes] = jnp.transpose(corr[kind, lanes, :])[0:COLS, :] - power_term

    row = lax.broadcasted_iota(jnp.int32, (ORIENTS, 128), 0).astype(F32)
    wide[32:56, :] = aux[1, 0, 0:24, :] + aux[1, 1, 0:24, :]
    turn(1, next_scores)

    def candidates(source, base, first, last):
        def few_step(j, carry):
            chosen = wide[pl.ds(base + j, 1), :] == row
            for h in range(NH):
                for tile in range(5):
                    part = source[h * ORIENTS:(h + 1) * ORIENTS, tile * 128:tile * 128 + 128]
                    value = jnp.sum(jnp.where(chosen, part, 0.0), axis=0, keepdims=True)
                    few[h * 5 + tile, pl.ds(j, 1), :] = value
            return carry

        lax.fori_loop(first, last, few_step, 0)

    sent = []
    for part, index in ((0, SCORE), (1, SCORE_2)):
        candidates(next_scores, 32, part * 8, part * 8 + 8)
        cut = pl.ds(part * 8, 8)
        sent.append(copy(index, few.at[:, cut, :], few_in.at[:, cut, :], beside))
        sent[-1].start()
    score(last, (0,))
    turn(0, expo)

    info = aux[0, 0, 0:24, :] + aux[0, 1, 0:24, :]
    wide[64:88, :] = info
    allowed = jnp.zeros((ORIENTS, 128), jnp.bool_)
    for j in range(CANDS):
        allowed = allowed | (info[j:j + 1, :] == row)
    allowed = jnp.where(allowed, 1.0, 0.0)
    allowed = jnp.concatenate([allowed] * NH, axis=0) > 0.5
    lower = lax.broadcasted_iota(jnp.int32, (COLS, 128), 1) < PAIR
    live = info[CANDS:CANDS + 1, :]
    least = jnp.float32(-3.0e38)
    arrived(SCORE, few_in.at[:, pl.ds(0, 8), :])
    arrived(SCORE_2, few_in.at[:, pl.ds(8, 8), :])

    def spread(h, source, base):
        added = [jnp.zeros((ORIENTS, 128), F32) for _ in range(5)]
        for j in range(CANDS):
            chosen = wide[base + j:base + j + 1, :] == row
            for tile in range(5):
                value = source[h * 5 + tile, j:j + 1, :]
                added[tile] = jnp.where(chosen, value, added[tile])
        return added

    def class_rows(h):
        return pl.ds(pl.multiple_of(h * ORIENTS, 16), ORIENTS)

    def spread_step(h, carry):
        for tile, added in enumerate(spread(h, few_in, 64)):
            expo[class_rows(h), tile * 128:tile * 128 + 128] += added
        return carry

    lax.fori_loop(0, NH, spread_step, 0)
    highest = jnp.full((1, 128), least, F32)
    for tile in range(5):
        lanes = slice(tile * 128, tile * 128 + 128)
        valid = allowed & lower if tile == 4 else allowed
        scores = jnp.where(valid, expo[:, lanes], least)
        highest = jnp.maximum(highest, jnp.max(scores, axis=0, keepdims=True))
    highest = jnp.maximum(highest, pltpu.roll(highest, 64, 1))
    partition = jnp.zeros((1, 128), F32)
    for tile in range(5):
        lanes = slice(tile * 128, tile * 128 + 128)
        valid = allowed & lower if tile == 4 else allowed
        terms = jnp.where(valid, jnp.exp(expo[:, lanes] - highest), 0.0)
        expo[:, lanes] = terms
        partition = partition + jnp.sum(terms, axis=0, keepdims=True)
    partition = partition + pltpu.roll(partition, 64, 1)

    norm[core, 0:1, :] = highest
    norm[core, 1:2, :] = partition
    norm[core, 2:8, :] = jnp.zeros((6, 128), F32)
    send(NORM, norm.at[core], norm.at[core], partner)
    arrived(NORM, norm.at[1 - core])
    other = norm[1 - core]
    peak = jnp.maximum(highest, other[0:1, :])
    mine_scale = jnp.exp(highest - peak)
    whole = partition * mine_scale + other[1:2, :] * jnp.exp(other[0:1, :] - peak)
    scale = jnp.where(live > 0.5, mine_scale / whole, 0.0)
    mass = jnp.zeros((COLS, 128), F32)
    for tile in range(5):
        lanes = slice(tile * 128, tile * 128 + 128)
        posterior = (expo[:, lanes] * scale).astype(BF16).astype(F32)
        mass = mass + posterior
        expo[:, lanes] = posterior
        if tile == 4:
            mass = mass + pltpu.roll(mass, 64, 1)
            posterior = jnp.where(lower, posterior, mass)
        post[:, lanes] = posterior.astype(BF16)
    for item in sent:
        item.wait_send()
    candidates(expo, 64, 0, CANDS)
    few_post[...] = few[...].astype(BF16)
    send(POST, few_post, few_post_in, beside)
    evidence = jnp.where(live > 0.5, peak + jnp.log(whole), 0.0)
    evidence = pltpu.roll(jnp.broadcast_to(evidence, evid_ref.shape), lax.rem(128 - core * SLAB, 128), 1)
    evid_ref[...] = evidence

    def project(weights, block):
        data = lax.dot_general(
            weights[...], shifted[block], contract_plain, preferred_element_type=F32
        )
        weight = lax.dot_general(
            weights[:, 512:640], ctf[block], contract_plain, preferred_element_type=F32
        )
        return data, weight

    def place(r):
        return ring4(y, r // 4) * 4 + ring4(x, lax.rem(r, 4))

    def own_step(r, carry):
        data, weight = project(post, place(r))
        acc[r, :, 0:256] = data
        acc[r, :, 256:384] = weight
        return carry

    def next_step(r):
        data, weight = project(post_z, 16 + place(r))
        acc[r, :, 0:256] += data
        acc[r, :, 256:384] += weight

    lax.fori_loop(0, 16, own_step, 0)
    arrived(POST, few_post_in)
    few_in[...] = few_post_in[...].astype(F32)
    lower_part = lax.broadcasted_iota(jnp.int32, (ORIENTS, 128), 1) < PAIR

    def spread_post(h, carry):
        mass = jnp.zeros((ORIENTS, 128), F32)
        for tile, value in enumerate(spread(h, few_in, 32)):
            mass = mass + value
            if tile == 4:
                mass = mass + pltpu.roll(mass, 64, 1)
                value = jnp.where(lower_part, value, mass)
            post_z[class_rows(h), tile * 128:tile * 128 + 128] = value.astype(BF16)
        return carry

    lax.fori_loop(0, NH, spread_post, 0)

    edge = COLS // 2

    def pack(half, slot, i, target, other, added=None):
        rows = slice(half * edge, half * edge + edge)
        value = acc[other * 4 + target if half == 0 else target * 4 + other, rows, :]
        if added is not None:
            value = value + recv1[half, added, i].astype(F32)
        send1[half, slot, i] = value.astype(BF16)

    def piece(half, slot, target, first):
        for i in (0, 1):
            pack(half, slot, i, target, first + i)
        send(
            RS_1 + 8 * half + slot, send1.at[half, slot], recv1.at[half, slot],
            along(half, 1 if slot % 2 == 0 else -1),
        )

    def piece_sum(half, slot, i, target, other, added):
        pack(half, slot, i, target, other, added)
        send(
            RS_1 + 8 * half + 2 * slot - 4 + i, send1.at[half, slot, i], recv1.at[half, slot, i],
            along(half, 1 if slot % 2 == 0 else -1),
        )

    def loop(count, index):
        def step(k, carry):
            next_step(index(k))
            return carry

        lax.fori_loop(0, count, step, 0)

    loop(4, lambda k: k * 4 + 2)
    piece(0, 0, 2, 0)
    piece(0, 1, 2, 2)
    loop(3, lambda k: 8 + k + k // 2)
    piece(1, 0, 2, 0)
    piece(1, 1, 2, 2)
    loop(9, lambda k: (k // 3 + k // 6) * 4 + lax.rem(k, 3) + lax.rem(k, 3) // 2)
    for half in (0, 1):
        piece(half, 2, 1, 2)
        piece(half, 3, 3, 0)
    for half in (0, 1):
        arrived(RS_1 + 8 * half + 1, recv1.at[half, 1])
        piece_sum(half, 5, 0, 3, 2, 1)
        arrived(RS_1 + 8 * half, recv1.at[half, 0])
        piece_sum(half, 4, 1, 1, 1, 0)
    for half in (0, 1):
        piece_sum(half, 5, 1, 3, 3, 1)
        piece_sum(half, 4, 0, 1, 0, 0)

    def relay_rows(half, top):
        start = half * edge + top * ORIENTS
        return slice(start, start + ORIENTS)

    def relay(half, slot, distance, top, added=None):
        r = distance * 4 if half == 0 else distance
        value = acc[r, relay_rows(half, top), :]
        if added is not None:
            arrived(RS_2 + 6 * half + added, recv2.at[half, added])
            value = value + recv2[half, added]
        send2[half, slot] = value
        send(
            RS_2 + 6 * half + slot, send2.at[half, slot], recv2.at[half, slot],
            along(1 - half, 1 if slot % 2 == 0 else -1),
        )

    def first_sum(other):
        i = other % 2
        whole_slot, split_slot = (3, 4) if other < 2 else (2, 5)
        for half in (0, 1):
            rows = slice(half * edge, half * edge + edge)
            if other in (1, 2):
                arrived(RS_1 + 8 * half + whole_slot, recv1.at[half, whole_slot])
            arrived(RS_1 + 8 * half + 2 * split_slot - 4 + i, recv1.at[half, split_slot, i])
            r = other * 4 if half == 0 else other
            acc[r, rows, :] += (
                recv1[half, whole_slot, i].astype(F32) + recv1[half, split_slot, i].astype(F32)
            )
            if other == 2:
                relay(half, 0, 2, 0)
                relay(half, 1, 2, 1)
            elif other == 1:
                relay(half, 2, 1, 1)
            elif other == 3:
                relay(half, 3, 3, 0)

    for other in (2, 1, 3):
        first_sum(other)
    for half in (0, 1):
        relay(half, 4, 1, 0, 0)
        relay(half, 5, 3, 1, 1)
    first_sum(0)

    for half in (0, 1):
        for slot in range(2, 6):
            arrived(RS_2 + 6 * half + slot, recv2.at[half, slot])
        sums2[half * 2] = acc[0, relay_rows(half, 0), :] + recv2[half, 3] + recv2[half, 4]
        sums2[half * 2 + 1] = acc[0, relay_rows(half, 1), :] + recv2[half, 2] + recv2[half, 5]

    middle = ORIENTS // 2

    def pass_on(slot, distance, top, added=None):
        value = sums2[ring4(z_hi, distance), top * middle:(top + 1) * middle, :]
        if added is not None:
            arrived(RS_Z + added, recv3.at[added])
            value = value + recv3[added]
        send3[slot] = value
        to = along_z(1 if slot % 2 == 0 else -1)
        send(RS_Z + slot, send3.at[slot], recv3.at[slot], to)

    pass_on(0, 2, 0)
    pass_on(1, 2, 1)
    pass_on(2, 1, 1)
    pass_on(3, -1, 0)
    pass_on(4, 1, 0, 0)
    pass_on(5, -1, 1, 1)
    for slot in range(2, 6):
        arrived(RS_Z + slot, recv3.at[slot])
    for top in (0, 1):
        rows = slice(top * middle, (top + 1) * middle)
        near, far = ((3, 4), (2, 5))[top]
        total = sums2[z_hi, rows, :] + recv3[near] + recv3[far]
        divisor = total[:, 256:384] + WIENER_TERM
        est_ref[rows, 0:128] = total[:, 0:128] / divisor
        est_ref[rows, 128:256] = total[:, 128:256] / divisor

    for item in pending:
        item.wait_send()


def on_device(particles, defocus, orient, center, live, sigma2, projections):
    images = particles.reshape(SLAB, 2, 16, 2, 128).transpose(3, 1, 0, 2, 4).reshape(2, 2, SLAB, 2048)
    vmem = pl.BlockSpec(memory_space=pltpu.VMEM)
    estimate, evidence = pl.pallas_call(
        kernel,
        out_shape=(
            jax.ShapeDtypeStruct((ORIENTS, 256), F32),
            jax.ShapeDtypeStruct((8, 128), F32),
        ),
        in_specs=[vmem] * 7,
        out_specs=(vmem, vmem),
        scratch_shapes=[
            pltpu.VMEM((NY, NX, NH, ORIENTS, 256), BF16),
            pltpu.VMEM((2, 2, 2, SLAB, 2048), BF16),
            pltpu.VMEM((2, 2, 56, 128), F32),
            pltpu.VMEM((128, 128), F32),
            pltpu.VMEM((5, BLOCKS, 128), F32),
            pltpu.VMEM((2, 8, 128), F32),
            pltpu.VMEM((32, ROWS, 256), BF16),
            pltpu.VMEM((32, 128, 128), BF16),
            pltpu.VMEM((2, ROWS, 256), F32),
            pltpu.VMEM((2, COLS, 128), F32),
            pltpu.VMEM((COLS, ROWS), F32),
            pltpu.VMEM((COLS, ROWS), F32),
            pltpu.VMEM((5 * NH, CANDS, 128), F32),
            pltpu.VMEM((5 * NH, CANDS, 128), F32),
            pltpu.VMEM((5 * NH, CANDS, 128), BF16),
            pltpu.VMEM((5 * NH, CANDS, 128), BF16),
            pltpu.VMEM((COLS, ROWS), BF16),
            pltpu.VMEM((COLS, ROWS), BF16),
            pltpu.VMEM((16, COLS, 384), F32),
            pltpu.VMEM((2, 6, 2, COLS // 2, 384), BF16),
            pltpu.VMEM((2, 6, 2, COLS // 2, 384), BF16),
            pltpu.VMEM((2, 6, ORIENTS, 384), F32),
            pltpu.VMEM((2, 6, ORIENTS, 384), F32),
            pltpu.VMEM((NH, ORIENTS, 384), F32),
            pltpu.VMEM((6, ORIENTS // 2, 384), F32),
            pltpu.VMEM((6, ORIENTS // 2, 384), F32),
            pltpu.SemaphoreType.DMA((COPIES,)),
            pltpu.SemaphoreType.DMA((COPIES,)),
            pltpu.SemaphoreType.DMA((2,)),
        ],
        compiler_params=pltpu.CompilerParams(
            collective_id=0, has_side_effects=True, vmem_limit_bytes=50 * 1024 * 1024
        ),
    )(
        images, orient.T, center.reshape(1, SLAB), defocus.reshape(1, SLAB), live.reshape(1, 1),
        sigma2.reshape(BLOCKS, 128), projections.reshape(ORIENTS, 256),
    )
    return (estimate.reshape(1, ORIENTS, 2, 128), evidence[0, 0:SLAB])


def solution(mesh):
    return jax.shard_map(
        on_device,
        mesh=mesh,
        in_specs=(
            P(("dom", "cls"), None, None),
            P(("dom", "cls")),
            P(("dom", "cls"), None),
            P(("dom", "cls")),
            P(("dom", "cls")),
            P(),
            P("cls", None, None, "dom"),
        ),
        out_specs=(P("cls", None, None, "dom"), P(("dom", "cls"))),
        check_vma=False,
    )
```

```python
import math

import jax
import jax.numpy as jnp
from jax import lax
from jax.experimental import pallas as pl
from jax.experimental.pallas import tpu as pltpu
from jax.sharding import PartitionSpec as P

FSIDE = 64
BOX = 128
GRID = 9
SHIFTS = 9
ORIENTS = 48
CANDS = 16
SLAB = 32

CTF_GAIN = 400.0
CTF_PHASE = 0.07
WIENER_TERM = 0.002

NX, NY, NH = 4, 4, 4
BLOCKS = 32
COLS = NH * ORIENTS
PAIR = 2 * SLAB
ROWS = 640
MESH = pl.DeviceIdType.MESH
F32, BF16 = jnp.float32, jnp.bfloat16

SIN_TERMS = (6.2831853025115025, -41.34170040531776, 81.60513138580835, -76.70301535406267,
             42.02592698764344, -14.899846674846755, 3.2381375198594955)
COS_TERMS = (0.9999999890590235, -19.73920449945402, 64.93911745989969, -85.45013953094733,
             60.16763095140483, -25.96759924996967, 6.5286581631738425)

AG_Z = 0
AG_2 = 3
AG_3 = 11
PART, PART_Z, PART_F = 35, 36, 37
AUX, AUX_Z, AUX_F = 38, 39, 40
SCORE, NORM, POST = 41, 42, 43
RS_1 = 44
RS_2 = 60
RS_Z = 72
COPIES = 78


def poly(terms, x):
    total = terms[-1] * x + terms[-2]
    for term in terms[-3::-1]:
        total = total * x + term
    return total


def sin_turns(t):
    return poly(SIN_TERMS, t * t) * t


def cos_turns(t):
    return poly(COS_TERMS, t * t)


def kernel(
    part_ref, orient_ref, center_ref, defocus_ref, live_ref, sigma_ref, proj_ref,
    est_ref, evid_ref,
    gath, imgs, aux, wide, tables, norm, shifted, ctf, corr, power_sum, expo, next_scores,
    few, few_in, few_post, few_post_in, post, post_z,
    acc, send1, recv1, send2, recv2, sums2, send3, recv3,
    send_sem, recv_sem, local_sem,
):
    dom, cls = lax.axis_index("dom"), lax.axis_index("cls")
    z_lo, x, y = lax.rem(dom, 2), lax.rem(dom // 2, 4), dom // 8
    core, z_hi = lax.rem(cls, 2), cls // 2
    z = z_hi * 2 + z_lo

    def device(yy, xx, zz):
        return ((yy * NX + xx) * 2 + lax.rem(zz, 2), (zz // 2) * 2 + core)

    def ring4(position, step):
        return lax.rem(position + step + 4, 4)

    def along(axis, step):
        if axis == 0:
            return device(y, ring4(x, step), z)
        return device(ring4(y, step), x, z)

    here = (x, y)
    partner = (dom, z_hi * 2 + 1 - core)
    beside = device(y, x, z_hi * 2 + 1 - z_lo)

    def along_z(step):
        return device(y, x, ring4(z_hi, step) * 2 + z_lo)

    def copy(index, source, target, to):
        return pltpu.make_async_remote_copy(
            src_ref=source, dst_ref=target, send_sem=send_sem.at[index],
            recv_sem=recv_sem.at[index], device_id=to, device_id_type=MESH,
        )

    pending = []

    def send(index, source, target, to):
        out = copy(index, source, target, to)
        out.start()
        pending.append(out)

    def arrived(index, target):
        copy(index, target, target, partner).wait_recv()

    barrier = pltpu.get_barrier_semaphore()
    friends = [partner, beside]
    friends += [along(axis, step) for axis in (0, 1) for step in (1, -1)]
    friends += [along_z(step) for step in range(1, NH)]
    for friend in friends:
        pl.semaphore_signal(barrier, inc=1, device_id=friend, device_id_type=MESH)

    own = [
        pltpu.make_async_copy(part_ref.at[z_lo], imgs.at[0, core], local_sem.at[0]),
        pltpu.make_async_copy(proj_ref, gath.at[y, x, z_hi], local_sem.at[1]),
    ]
    for item in own:
        item.start()
    pl.semaphore_wait(barrier, len(friends))

    mine = gath.at[y, x, z_hi]
    for step in range(1, NH):
        send(AG_Z + step - 1, proj_ref, mine, along_z(step))
    send(PART, part_ref.at[z_lo], imgs.at[0, core], partner)

    center = center_ref[...].astype(F32)
    center_y = jnp.floor((center + 0.5) * (1.0 / (GRID - 2)))
    center_x = center - center_y * (GRID - 2)
    slot = lax.broadcasted_iota(jnp.int32, (1, SLAB), 1)
    wide[...] = jnp.zeros_like(wide)
    wide[0:CANDS, 0:SLAB] = orient_ref[...].astype(F32)
    wide[16:17, 0:SLAB] = jnp.where(slot < live_ref[...], 1.0, 0.0)
    wide[17:18, 0:SLAB] = CTF_GAIN * defocus_ref[...].astype(F32)
    wide[18:19, 0:SLAB] = center_x + (1 - GRID // 2)
    wide[19:20, 0:SLAB] = center_y + (1 - GRID // 2)
    placed = pltpu.roll(wide[0:24, :], core * SLAB, 1)
    aux[0, core, 0:24, :] = placed + pltpu.roll(placed, 64, 1)
    aux[0, core, 24:56, :] = jnp.transpose(wide[...])[0:SLAB, :]
    send(AUX, aux.at[0, core], aux.at[0, core], partner)
    send(AUX_Z, aux.at[0, core], aux.at[1, core], beside)

    block_row = lax.broadcasted_iota(jnp.int32, (BLOCKS, 128), 0)
    lane = lax.broadcasted_iota(jnp.int32, (BLOCKS, 128), 1)
    v_all = (block_row * 2 + lane // FSIDE - FSIDE // 2).astype(F32)
    u_all = lax.rem(lane, FSIDE).astype(F32)
    tables[0] = (u_all * u_all + v_all * v_all) * (1.0 / (BOX * BOX))
    tables[1] = v_all
    tables[2] = cos_turns(v_all * (1.0 / BOX))
    tables[3] = sin_turns(v_all * (1.0 / BOX))
    tables[4] = 1.0 / sigma_ref[...]
    u = u_all[0:1, :]
    cos_u, sin_u = cos_turns(u * (1.0 / BOX)), sin_turns(u * (1.0 / BOX))
    for item in own:
        item.wait()

    def shift_tile(group, owner, tile):
        start = tile * 16
        info = aux[group, owner, 24 + start:40 + start, :]
        gain, t_x, t_y = info[:, 17:18], info[:, 18:19], info[:, 19:20]
        base_turn = u * t_x
        row0 = owner * SLAB + start

        def rows_at(base):
            return pl.ds(pl.multiple_of(base + row0, 16), 16)

        def step(at_yx, carry):
            d = at_yx * 2 + z_lo
            block = group * 16 + at_yx
            radius = tables[0, pl.ds(d, 1), :]
            v = tables[1, pl.ds(d, 1), :]
            cos_v = tables[2, pl.ds(d, 1), :]
            sin_v = tables[3, pl.ds(d, 1), :]
            inverse = tables[4, pl.ds(d, 1), :]
            lanes = pl.ds(pl.multiple_of(at_yx * 128, 128), 128)
            real = imgs[group, owner, 0, pl.ds(start, 16), lanes].astype(F32)
            imag = imgs[group, owner, 1, pl.ds(start, 16), lanes].astype(F32)
            angle = gain * radius + CTF_PHASE
            turns = jnp.floor(angle * (0.5 / math.pi) + 0.5)
            rest = (angle - turns * 6.28125) - turns * 0.0019353071795864769
            contrast = -sin_turns(rest * (0.5 / math.pi))
            weight = contrast * inverse
            ctf_weight = (contrast * contrast * inverse).astype(BF16)
            ctf[block, rows_at(PAIR), :] = ctf_weight
            turn = (base_turn + v * t_y) * (1.0 / BOX)
            turn = turn - jnp.floor(turn + 0.5)
            cosine, sine = cos_turns(turn), sin_turns(turn)
            real, imag = real * weight, imag * weight
            mid = (real * cosine - imag * sine, real * sine + imag * cosine)

            def rotations(value, cos_, sin_):
                re, im = value
                re_c, re_s, im_c, im_s = re * cos_, re * sin_, im * cos_, im * sin_
                return ((re_c + im_s, im_c - re_s), value, (re_c - im_s, im_c + re_s))

            for d_y, moved in enumerate(rotations(mid, cos_v, sin_v)):
                for d_x, (re, im) in enumerate(rotations(moved, cos_u, sin_u)):
                    at = rows_at((d_y * 3 + d_x) * PAIR)
                    shifted[block, at, 0:128] = re.astype(BF16)
                    shifted[block, at, 128:256] = im.astype(BF16)
            return carry

        lax.fori_loop(0, 16, step, 0, unroll=8)

    def zero_step(block, carry):
        shifted[block, SHIFTS * PAIR:, :] = jnp.zeros((ROWS - SHIFTS * PAIR, 256), BF16)
        ctf[block, 0:PAIR, :] = jnp.zeros((PAIR, 128), BF16)
        return carry

    def view(half, position, part=None):
        cut = pl.ds(half * 2, 2) if part is None else pl.ds(half * 2 + part, 1)
        if half == 0:
            return gath.at[y, position, cut]
        return gath.at[position, x, cut]

    def view_piece(half, piece, position):
        cut = pl.ds(half * 2, 2)
        if half == 0:
            return gath.at[position, ring4(x, piece), cut]
        return gath.at[ring4(y, piece), position, cut]

    def ring_first(half):
        ref = view(half, here[half])
        send(AG_2 + 4 * half, ref, ref, along(half, 1))
        send(AG_2 + 4 * half + 1, ref, ref, along(half, -1))

    def ring_second(half):
        base = AG_2 + 4 * half
        left, right = ring4(here[half], -1), ring4(here[half], 1)
        arrived(base, view(half, left))
        ref = view(half, left, 0)
        send(base + 2, ref, ref, along(half, 1))
        arrived(base + 1, view(half, right))
        ref = view(half, right, 1)
        send(base + 3, ref, ref, along(half, -1))

    def ring_end(half):
        far = ring4(here[half], 2)
        arrived(AG_2 + 4 * half + 2, view(half, far, 0))
        arrived(AG_2 + 4 * half + 3, view(half, far, 1))

    def piece_first(half, piece):
        axis = 1 - half
        base = AG_3 + 12 * half + 3 * piece
        ref = view_piece(half, piece, here[axis])
        send(base, ref, ref, along(axis, 1))
        send(base + 1, ref, ref, along(axis, -1))

    def piece_second(half, piece):
        axis = 1 - half
        base = AG_3 + 12 * half + 3 * piece
        left = view_piece(half, piece, ring4(here[axis], -1))
        right = view_piece(half, piece, ring4(here[axis], 1))
        if piece % 2 == 0:
            arrived(base, left)
            send(base + 2, left, left, along(axis, 1))
            arrived(base + 1, right)
        else:
            arrived(base + 1, right)
            send(base + 2, right, right, along(axis, -1))
            arrived(base, left)

    def piece_end(half, piece):
        axis = 1 - half
        far = view_piece(half, piece, ring4(here[axis], 2))
        arrived(AG_3 + 12 * half + 3 * piece + 2, far)

    contract_last = (((1,), (1,)), ((), ()))
    contract_plain = (((1,), (0,)), ((), ()))

    def score(blocks, kinds=(0, 1)):
        volumes = [gath[yy, xx].reshape(COLS, 256) for yy, xx in blocks]
        squares = []
        for volume in volumes:
            re, im = volume[:, 0:128].astype(F32), volume[:, 128:256].astype(F32)
            squares.append((re * re + im * im).astype(BF16))
        for kind in kinds:
            total = power = None
            for (yy, xx), volume, squared in zip(blocks, volumes, squares):
                block = kind * 16 + yy * 4 + xx
                term = lax.dot_general(
                    shifted[block], volume, contract_last, preferred_element_type=F32
                )
                term_p = lax.dot_general(
                    squared, ctf[block], contract_last, preferred_element_type=F32
                )
                total = term if total is None else total + term
                power = term_p if power is None else power + term_p
            corr[kind, :, 0:COLS] += total
            power_sum[kind] += power

    def near_step(k, carry):
        yy = ring4(y, k + k // 2)
        score([(yy, ring4(x, dx)) for dx in (0, 1, 3)])
        return carry

    def far_step(k, carry):
        step = k + k // 2
        score([(ring4(y, step), ring4(x, 2)), (ring4(y, 2), ring4(x, step))])
        return carry

    shift_tile(0, core, 0)
    shift_tile(0, core, 1)
    lax.fori_loop(0, 32, zero_step, 0)
    corr[...] = jnp.zeros_like(corr)
    power_sum[...] = jnp.zeros_like(power_sum)
    for step in range(1, NH):
        arrived(AG_Z + step - 1, gath.at[y, x, ring4(z_hi, -step)])
    for half in (0, 1):
        ring_first(half)
    for half in (0, 1):
        piece_first(half, 0)
    send(PART_Z, part_ref.at[1 - z_lo], imgs.at[1, core], beside)
    arrived(PART, imgs.at[0, 1 - core])
    arrived(AUX, aux.at[0, 1 - core])
    shift_tile(0, 1 - core, 0)
    for half in (0, 1):
        ring_second(half)
    for half in (0, 1):
        piece_first(half, 1)
        piece_first(half, 3)
    shift_tile(0, 1 - core, 1)
    for half in (0, 1):
        ring_end(half)
        piece_first(half, 2)
    for half in (0, 1):
        piece_second(half, 0)
    arrived(PART_Z, imgs.at[1, core])
    send(PART_F, imgs.at[1, core], imgs.at[1, core], partner)
    arrived(AUX_Z, aux.at[1, core])
    send(AUX_F, aux.at[1, core], aux.at[1, core], partner)
    shift_tile(1, core, 0)
    for half in (0, 1):
        piece_second(half, 1)
        piece_second(half, 3)
    shift_tile(1, core, 1)
    arrived(PART_F, imgs.at[1, 1 - core])
    arrived(AUX_F, aux.at[1, 1 - core])
    shift_tile(1, 1 - core, 0)
    for half in (0, 1):
        piece_second(half, 2)
    shift_tile(1, 1 - core, 1)
    lax.fori_loop(0, 3, near_step, 0)
    for half in (0, 1):
        for piece in (0, 1, 3):
            piece_end(half, piece)
    lax.fori_loop(0, 3, far_step, 0)
    for half in (0, 1):
        piece_end(half, 2)
    last = [(ring4(y, 2), ring4(x, 2))]
    score(last, (1,))

    def turn(kind, target):
        power_term = 0.5 * (power_sum[kind] + pltpu.roll(power_sum[kind], 64, 1))
        for tile in range(5):
            lanes = slice(tile * 128, tile * 128 + 128)
            target[:, lanes] = jnp.transpose(corr[kind, lanes, :])[0:COLS, :] - power_term

    row = lax.broadcasted_iota(jnp.int32, (ORIENTS, 128), 0).astype(F32)
    wide[32:56, :] = aux[1, 0, 0:24, :] + aux[1, 1, 0:24, :]
    turn(1, next_scores)

    def candidates(source, base):
        def few_step(j, carry):
            chosen = wide[pl.ds(base + j, 1), :] == row
            for h in range(NH):
                for tile in range(5):
                    part = source[h * ORIENTS:(h + 1) * ORIENTS, tile * 128:tile * 128 + 128]
                    value = jnp.sum(jnp.where(chosen, part, 0.0), axis=0, keepdims=True)
                    few[h * 5 + tile, pl.ds(j, 1), :] = value
            return carry

        lax.fori_loop(0, CANDS, few_step, 0)

    candidates(next_scores, 32)
    score_sent = copy(SCORE, few, few_in, beside)
    score_sent.start()
    score(last, (0,))
    turn(0, expo)

    info = aux[0, 0, 0:24, :] + aux[0, 1, 0:24, :]
    wide[64:88, :] = info
    allowed = jnp.zeros((ORIENTS, 128), jnp.bool_)
    for j in range(CANDS):
        allowed = allowed | (info[j:j + 1, :] == row)
    allowed = jnp.where(allowed, 1.0, 0.0)
    allowed = jnp.concatenate([allowed] * NH, axis=0) > 0.5
    lower = lax.broadcasted_iota(jnp.int32, (COLS, 128), 1) < PAIR
    live = info[CANDS:CANDS + 1, :]
    least = jnp.float32(-3.0e38)
    arrived(SCORE, few_in)

    def spread(h, source, base):
        added = [jnp.zeros((ORIENTS, 128), F32) for _ in range(5)]
        for j in range(CANDS):
            chosen = wide[base + j:base + j + 1, :] == row
            for tile in range(5):
                value = source[h * 5 + tile, j:j + 1, :]
                added[tile] = jnp.where(chosen, value, added[tile])
        return added

    def class_rows(h):
        return pl.ds(pl.multiple_of(h * ORIENTS, 16), ORIENTS)

    def spread_step(h, carry):
        for tile, added in enumerate(spread(h, few_in, 64)):
            expo[class_rows(h), tile * 128:tile * 128 + 128] += added
        return carry

    lax.fori_loop(0, NH, spread_step, 0)
    highest = jnp.full((1, 128), least, F32)
    for tile in range(5):
        lanes = slice(tile * 128, tile * 128 + 128)
        valid = allowed & lower if tile == 4 else allowed
        scores = jnp.where(valid, expo[:, lanes], least)
        highest = jnp.maximum(highest, jnp.max(scores, axis=0, keepdims=True))
    highest = jnp.maximum(highest, pltpu.roll(highest, 64, 1))
    partition = jnp.zeros((1, 128), F32)
    for tile in range(5):
        lanes = slice(tile * 128, tile * 128 + 128)
        valid = allowed & lower if tile == 4 else allowed
        terms = jnp.where(valid, jnp.exp(expo[:, lanes] - highest), 0.0)
        expo[:, lanes] = terms
        partition = partition + jnp.sum(terms, axis=0, keepdims=True)
    partition = partition + pltpu.roll(partition, 64, 1)

    norm[core, 0:1, :] = highest
    norm[core, 1:2, :] = partition
    norm[core, 2:8, :] = jnp.zeros((6, 128), F32)
    send(NORM, norm.at[core], norm.at[core], partner)
    arrived(NORM, norm.at[1 - core])
    other = norm[1 - core]
    peak = jnp.maximum(highest, other[0:1, :])
    mine_scale = jnp.exp(highest - peak)
    whole = partition * mine_scale + other[1:2, :] * jnp.exp(other[0:1, :] - peak)
    scale = jnp.where(live > 0.5, mine_scale / whole, 0.0)
    mass = jnp.zeros((COLS, 128), F32)
    for tile in range(5):
        lanes = slice(tile * 128, tile * 128 + 128)
        posterior = (expo[:, lanes] * scale).astype(BF16).astype(F32)
        mass = mass + posterior
        expo[:, lanes] = posterior
        if tile == 4:
            mass = mass + pltpu.roll(mass, 64, 1)
            posterior = jnp.where(lower, posterior, mass)
        post[:, lanes] = posterior.astype(BF16)
    score_sent.wait_send()
    candidates(expo, 64)
    few_post[...] = few[...].astype(BF16)
    send(POST, few_post, few_post_in, beside)
    evidence = jnp.where(live > 0.5, peak + jnp.log(whole), 0.0)
    evidence = pltpu.roll(jnp.broadcast_to(evidence, evid_ref.shape), lax.rem(128 - core * SLAB, 128), 1)
    evid_ref[...] = evidence

    def project(weights, block):
        data = lax.dot_general(
            weights[...], shifted[block], contract_plain, preferred_element_type=F32
        )
        weight = lax.dot_general(
            weights[:, 512:640], ctf[block], contract_plain, preferred_element_type=F32
        )
        return data, weight

    def place(r):
        return ring4(y, r // 4) * 4 + ring4(x, lax.rem(r, 4))

    def own_step(r, carry):
        data, weight = project(post, place(r))
        acc[r, :, 0:256] = data
        acc[r, :, 256:384] = weight
        return carry

    def next_step(r):
        data, weight = project(post_z, 16 + place(r))
        acc[r, :, 0:256] += data
        acc[r, :, 256:384] += weight

    lax.fori_loop(0, 16, own_step, 0)
    arrived(POST, few_post_in)
    few_in[...] = few_post_in[...].astype(F32)
    lower_part = lax.broadcasted_iota(jnp.int32, (ORIENTS, 128), 1) < PAIR

    def spread_post(h, carry):
        mass = jnp.zeros((ORIENTS, 128), F32)
        for tile, value in enumerate(spread(h, few_in, 32)):
            mass = mass + value
            if tile == 4:
                mass = mass + pltpu.roll(mass, 64, 1)
                value = jnp.where(lower_part, value, mass)
            post_z[class_rows(h), tile * 128:tile * 128 + 128] = value.astype(BF16)
        return carry

    lax.fori_loop(0, NH, spread_post, 0)

    edge = COLS // 2

    def pack(half, slot, i, target, other, added=None):
        rows = slice(half * edge, half * edge + edge)
        value = acc[other * 4 + target if half == 0 else target * 4 + other, rows, :]
        if added is not None:
            value = value + recv1[half, added, i].astype(F32)
        send1[half, slot, i] = value.astype(BF16)

    def piece(half, slot, target, first):
        for i in (0, 1):
            pack(half, slot, i, target, first + i)
        send(
            RS_1 + 8 * half + slot, send1.at[half, slot], recv1.at[half, slot],
            along(half, 1 if slot % 2 == 0 else -1),
        )

    def piece_sum(half, slot, i, target, other, added):
        pack(half, slot, i, target, other, added)
        send(
            RS_1 + 8 * half + 2 * slot - 4 + i, send1.at[half, slot, i], recv1.at[half, slot, i],
            along(half, 1 if slot % 2 == 0 else -1),
        )

    def loop(count, index):
        def step(k, carry):
            next_step(index(k))
            return carry

        lax.fori_loop(0, count, step, 0)

    loop(4, lambda k: k * 4 + 2)
    piece(0, 0, 2, 0)
    piece(0, 1, 2, 2)
    loop(3, lambda k: 8 + k + k // 2)
    piece(1, 0, 2, 0)
    piece(1, 1, 2, 2)
    loop(9, lambda k: (k // 3 + k // 6) * 4 + lax.rem(k, 3) + lax.rem(k, 3) // 2)
    for half in (0, 1):
        piece(half, 2, 1, 2)
        piece(half, 3, 3, 0)
    for half in (0, 1):
        arrived(RS_1 + 8 * half + 1, recv1.at[half, 1])
        piece_sum(half, 5, 0, 3, 2, 1)
        arrived(RS_1 + 8 * half, recv1.at[half, 0])
        piece_sum(half, 4, 1, 1, 1, 0)
    for half in (0, 1):
        piece_sum(half, 5, 1, 3, 3, 1)
        piece_sum(half, 4, 0, 1, 0, 0)

    def relay_rows(half, top):
        start = half * edge + top * ORIENTS
        return slice(start, start + ORIENTS)

    def relay(half, slot, distance, top, added=None):
        r = distance * 4 if half == 0 else distance
        value = acc[r, relay_rows(half, top), :]
        if added is not None:
            arrived(RS_2 + 6 * half + added, recv2.at[half, added])
            value = value + recv2[half, added]
        send2[half, slot] = value
        send(
            RS_2 + 6 * half + slot, send2.at[half, slot], recv2.at[half, slot],
            along(1 - half, 1 if slot % 2 == 0 else -1),
        )

    def first_sum(other):
        i = other % 2
        whole_slot, split_slot = (3, 4) if other < 2 else (2, 5)
        for half in (0, 1):
            rows = slice(half * edge, half * edge + edge)
            if other in (1, 2):
                arrived(RS_1 + 8 * half + whole_slot, recv1.at[half, whole_slot])
            arrived(RS_1 + 8 * half + 2 * split_slot - 4 + i, recv1.at[half, split_slot, i])
            r = other * 4 if half == 0 else other
            acc[r, rows, :] += (
                recv1[half, whole_slot, i].astype(F32) + recv1[half, split_slot, i].astype(F32)
            )
            if other == 2:
                relay(half, 0, 2, 0)
                relay(half, 1, 2, 1)
            elif other == 1:
                relay(half, 2, 1, 1)
            elif other == 3:
                relay(half, 3, 3, 0)

    for other in (2, 1, 3):
        first_sum(other)
    for half in (0, 1):
        relay(half, 4, 1, 0, 0)
        relay(half, 5, 3, 1, 1)
    first_sum(0)

    for half in (0, 1):
        for slot in range(2, 6):
            arrived(RS_2 + 6 * half + slot, recv2.at[half, slot])
        sums2[half * 2] = acc[0, relay_rows(half, 0), :] + recv2[half, 3] + recv2[half, 4]
        sums2[half * 2 + 1] = acc[0, relay_rows(half, 1), :] + recv2[half, 2] + recv2[half, 5]

    middle = ORIENTS // 2

    def pass_on(slot, distance, top, added=None):
        value = sums2[ring4(z_hi, distance), top * middle:(top + 1) * middle, :]
        if added is not None:
            arrived(RS_Z + added, recv3.at[added])
            value = value + recv3[added]
        send3[slot] = value
        to = along_z(1 if slot % 2 == 0 else -1)
        send(RS_Z + slot, send3.at[slot], recv3.at[slot], to)

    pass_on(0, 2, 0)
    pass_on(1, 2, 1)
    pass_on(2, 1, 1)
    pass_on(3, -1, 0)
    pass_on(4, 1, 0, 0)
    pass_on(5, -1, 1, 1)
    for slot in range(2, 6):
        arrived(RS_Z + slot, recv3.at[slot])
    for top in (0, 1):
        rows = slice(top * middle, (top + 1) * middle)
        near, far = ((3, 4), (2, 5))[top]
        total = sums2[z_hi, rows, :] + recv3[near] + recv3[far]
        divisor = total[:, 256:384] + WIENER_TERM
        est_ref[rows, 0:128] = total[:, 0:128] / divisor
        est_ref[rows, 128:256] = total[:, 128:256] / divisor

    for item in pending:
        item.wait_send()


def on_device(particles, defocus, orient, center, live, sigma2, projections):
    images = particles.reshape(SLAB, 2, 16, 2, 128).transpose(3, 1, 0, 2, 4).reshape(2, 2, SLAB, 2048)
    vmem = pl.BlockSpec(memory_space=pltpu.VMEM)
    estimate, evidence = pl.pallas_call(
        kernel,
        out_shape=(
            jax.ShapeDtypeStruct((ORIENTS, 256), F32),
            jax.ShapeDtypeStruct((8, 128), F32),
        ),
        in_specs=[vmem] * 7,
        out_specs=(vmem, vmem),
        scratch_shapes=[
            pltpu.VMEM((NY, NX, NH, ORIENTS, 256), BF16),
            pltpu.VMEM((2, 2, 2, SLAB, 2048), BF16),
            pltpu.VMEM((2, 2, 56, 128), F32),
            pltpu.VMEM((128, 128), F32),
            pltpu.VMEM((5, BLOCKS, 128), F32),
            pltpu.VMEM((2, 8, 128), F32),
            pltpu.VMEM((32, ROWS, 256), BF16),
            pltpu.VMEM((32, 128, 128), BF16),
            pltpu.VMEM((2, ROWS, 256), F32),
            pltpu.VMEM((2, COLS, 128), F32),
            pltpu.VMEM((COLS, ROWS), F32),
            pltpu.VMEM((COLS, ROWS), F32),
            pltpu.VMEM((5 * NH, CANDS, 128), F32),
            pltpu.VMEM((5 * NH, CANDS, 128), F32),
            pltpu.VMEM((5 * NH, CANDS, 128), BF16),
            pltpu.VMEM((5 * NH, CANDS, 128), BF16),
            pltpu.VMEM((COLS, ROWS), BF16),
            pltpu.VMEM((COLS, ROWS), BF16),
            pltpu.VMEM((16, COLS, 384), F32),
            pltpu.VMEM((2, 6, 2, COLS // 2, 384), BF16),
            pltpu.VMEM((2, 6, 2, COLS // 2, 384), BF16),
            pltpu.VMEM((2, 6, ORIENTS, 384), F32),
            pltpu.VMEM((2, 6, ORIENTS, 384), F32),
            pltpu.VMEM((NH, ORIENTS, 384), F32),
            pltpu.VMEM((6, ORIENTS // 2, 384), F32),
            pltpu.VMEM((6, ORIENTS // 2, 384), F32),
            pltpu.SemaphoreType.DMA((COPIES,)),
            pltpu.SemaphoreType.DMA((COPIES,)),
            pltpu.SemaphoreType.DMA((2,)),
        ],
        compiler_params=pltpu.CompilerParams(
            collective_id=0, has_side_effects=True, vmem_limit_bytes=50 * 1024 * 1024
        ),
    )(
        images, orient.T, center.reshape(1, SLAB), defocus.reshape(1, SLAB), live.reshape(1, 1),
        sigma2.reshape(BLOCKS, 128), projections.reshape(ORIENTS, 256),
    )
    return (estimate.reshape(1, ORIENTS, 2, 128), evidence[0, 0:SLAB])


def solution(mesh):
    return jax.shard_map(
        on_device,
        mesh=mesh,
        in_specs=(
            P(("dom", "cls"), None, None),
            P(("dom", "cls")),
            P(("dom", "cls"), None),
            P(("dom", "cls")),
            P(("dom", "cls")),
            P(),
            P("cls", None, None, "dom"),
        ),
        out_specs=(P("cls", None, None, "dom"), P(("dom", "cls"))),
        check_vma=False,
    )
```
